256 devices in a mesh: ex: 64 (over z, y, x_hi), feat: 4 (over x_lo, core).
Axes of the slice: x: 4 (x_hi: 2, x_lo: 2; x = x_hi * 2 + x_lo), y: 4, z: 8, core: 2. Of those that a mesh axis runs over, the one named last changes fastest.
Arguments:
- left_factors: bfloat16 [4, 1664, 4, 5120], P('feat', 'ex'), may hold values from -6 to 6
- right_factors: bfloat16 [4, 1664, 4, 5120], P('feat', 'ex'), may hold values from -6 to 6
- left_proj: bfloat16 [4, 5120, 32], P('feat'), may hold values from -0.078125 to 0.078125
- right_proj: bfloat16 [4, 5120, 64], P('feat'), may hold values from -0.078125 to 0.078125
- val_ids: int32 [256], replicated, may hold values from 0 to 1663
Outputs:
- weights: float32 [1664], P('ex')
- residual: float32 [1664], P('ex')
The draws below stay inside these ranges and needn't reach their ends.
Inputs may be any that keep to these rules, and one draw needn't show every extreme that they name: `val_ids`: ids of training examples; an id may repeat.
All inputs are finite; a program needn't handle non-finite values.
Results may differ from the reference program's by a relative error of at most 0.03.
Values may be sent and summed in bfloat16 or wider, within the bound.
A program may use at most 64 MiB of HBM per device.

```python
import math
import jax
import jax.numpy as jnp
from jax import lax

D = 5120
LAYERS = 4
RANK = 4
KA = 32
KB = 64
NVAL = 256
ITERS = 2
EXAMPLES = 1664
FEAT = 8192


def with_ends(drawn, rng, least, largest):
    longest = drawn.shape.index(max(drawn.shape))
    spots = []
    for shift in (0, 1):
        where = [jax.random.randint(jax.random.fold_in(rng, axis), (), 0, length) for axis, length in enumerate(drawn.shape)]
        where[longest] = (where[longest] + shift) % drawn.shape[longest]
        spots.append(tuple(where))
    return drawn.at[spots[0]].set(least).at[spots[1]].set(largest)


def steps_of(stream_key, extent, pieces, least, top_value):
    level, own = 1.0, jax.random.fold_in(stream_key, 6)
    for position, parts in pieces:
        heights = jnp.exp(jax.random.uniform(jax.random.fold_in(own, position), (parts,), jnp.float32, least / len(pieces), top_value / len(pieces)))
        level = level * jnp.repeat(heights, extent[position] // parts).reshape([-1 if axis == position else 1 for axis in range(len(extent))])
    return level


def normal_values(key, shape, width, most, shards=(), held_as=jnp.bfloat16):
    values = jax.random.normal(key, shape, jnp.float32) * width
    if len(shards) > 0:
        values = steps_of(key, shape, shards, -0.22, 0.18) * values
    return jnp.clip(values, min=-most, max=most).astype(held_as)


def setup_inputs(seed: int = 0) -> dict:
    keys = jax.random.split(jax.random.key(seed), 6)
    left_factors = normal_values(keys[0], (LAYERS, EXAMPLES, RANK, D), 1.0, 6.0, ((0, 4), (1, 64)))
    right_factors = normal_values(keys[1], (LAYERS, EXAMPLES, RANK, D), 1.0, 6.0, ((0, 4), (1, 64)))
    left_proj = normal_values(keys[2], (LAYERS, D, KA), D ** -0.5, 0.078125, ((0, 4),))
    right_proj = normal_values(keys[3], (LAYERS, D, KB), D ** -0.5, 0.078125, ((0, 4),))
    val_ids = with_ends(jax.random.randint(keys[4], (NVAL,), 0, EXAMPLES), jax.random.fold_in(keys[4], 1), 0, EXAMPLES - 1).astype(jnp.int32)
    return dict(left_factors=left_factors, right_factors=right_factors, left_proj=left_proj, right_proj=right_proj, val_ids=val_ids)


def reference(left_factors, right_factors, left_proj, right_proj, val_ids):
    blocks = []
    for layer in range(LAYERS):
        left_part = jnp.einsum('erd,dk->erk', left_factors[layer].astype(jnp.float32), left_proj[layer].astype(jnp.float32), precision=lax.Precision.HIGHEST)
        right_part = jnp.einsum('erd,dk->erk', right_factors[layer].astype(jnp.float32), right_proj[layer].astype(jnp.float32), precision=lax.Precision.HIGHEST)
        outer = jnp.einsum('erk,erm->ekm', left_part, right_part, precision=lax.Precision.HIGHEST) / math.sqrt(RANK)
        blocks.append(outer.reshape(EXAMPLES, KA * KB).astype(jnp.bfloat16))
    wide = jnp.concatenate(blocks, axis=1).astype(jnp.float32)
    counts = jnp.zeros((EXAMPLES,), jnp.float32).at[val_ids].add(1.0)
    target = jnp.dot(counts, wide, precision=lax.Precision.HIGHEST) / NVAL
    align = jnp.dot(wide, target, precision=lax.Precision.HIGHEST) * math.sqrt(NVAL / FEAT)

    def apply(vector):
        mixed = jnp.dot(vector, wide, precision=lax.Precision.HIGHEST)
        return jnp.dot(wide, mixed, precision=lax.Precision.HIGHEST) / FEAT + 0.5 * vector
    weights = jnp.zeros_like(align)
    residual = align
    direction = align
    norm_now = jnp.sum(residual * residual)
    for step in range(ITERS):
        image = apply(direction)
        alpha = norm_now / jnp.sum(direction * image)
        weights = weights + alpha * direction
        residual = residual - alpha * image
        norm_next = jnp.sum(residual * residual)
        direction = residual + norm_next / norm_now * direction
        norm_now = norm_next
    return (weights, residual)
```

```python
import functools
import math

import jax
import jax.numpy as jnp
from jax import lax
from jax.experimental import pallas as pl
from jax.experimental.pallas import tpu as pltpu
from jax.sharding import PartitionSpec as P

MESH = pl.DeviceIdType.MESH
NT = (((1,), (1,)), ((), ()))
NN = (((1,), (0,)), ((), ()))
SIZE = dict(z=8, y=4, xh=2, xl=2, c=2)
RIDGE = 0.5
CHUNKS = 4
LANES = 128


def coordinates():
    ex = lax.axis_index("ex")
    feat = lax.axis_index("feat")
    return dict(z=ex // 8, y=(ex // 2) % 4, xh=ex % 2, xl=feat // 2, c=feat % 2)


def device(at):
    return (at["z"] * 8 + at["y"] * 2 + at["xh"], at["xl"] * 2 + at["c"])


def moved(at, **steps):
    new = dict(at)
    for axis, step in steps.items():
        if step:
            new[axis] = (at[axis] + step) % SIZE[axis]
    return new


def hops(y, xh, xl):
    x = 2 * xh + xl
    return min(y, 4 - y) + min(x, 4 - x)


def split(value):
    high = value.astype(jnp.bfloat16)
    low = (value - high.astype(jnp.float32)).astype(jnp.bfloat16)
    return high, low


def pack(value):
    return jnp.concatenate([value[:16], value[16:]], axis=1)


def unpack(value):
    return jnp.concatenate([value[:, :64], value[:, 64:]], axis=0)


def dot(a, b, dims):
    return lax.dot_general(a, b, dims, preferred_element_type=jnp.float32)


def to_features(left, right, vector):
    both = jnp.concatenate(split(left.astype(jnp.float32) * vector), axis=0)
    sums = dot(both, right, NT)
    return pack(sums[:32] + sums[32:])


def kernel(
    rows, rank, total_features, val_count,
    lf_hbm, rf_hbm, lp_hbm, rp_hbm, ids_hbm, out_ref,
    lf, rf, lp, rp, ids, blocks, first, second, sums, pair,
    load_sem, ids_sem, send_sem, recv_sem,
):
    at = coordinates()
    width = lf_hbm.shape[3]
    step = width // CHUNKS
    used = rows * rank
    plane_slot = at["y"] * 2 + at["xh"]
    slot = at["xl"] * 8 + plane_slot

    loads = []
    for i in range(CHUNKS):
        part = pl.ds(i * step, step)
        group = [
            pltpu.make_async_copy(lp_hbm.at[0, :, part], lp.at[:, part], load_sem.at[i, 0]),
            pltpu.make_async_copy(lf_hbm.at[0, :, :, part], lf.at[i], load_sem.at[i, 1]),
            pltpu.make_async_copy(rp_hbm.at[0, :, part], rp.at[:, part], load_sem.at[i, 2]),
            pltpu.make_async_copy(rf_hbm.at[0, :, :, part], rf.at[i], load_sem.at[i, 3]),
        ]
        for copy in group:
            copy.start()
        loads.append(group)
    load_ids = pltpu.make_async_copy(ids_hbm, ids, ids_sem)
    load_ids.start()

    along_z = [moved(at, z=d) for d in (4, 3, 5, 2, 6, 1, 7)]
    plane = [(y, xh, xl) for y in range(4) for xh in range(2) for xl in range(2) if y or xh or xl]
    plane = [moved(at, y=y, xh=xh, xl=xl) for y, xh, xl in sorted(plane, key=lambda o: -hops(*o))]
    other = moved(at, c=1)
    barrier = pltpu.get_barrier_semaphore()
    for peer in along_z + plane + [other]:
        pl.semaphore_signal(barrier, inc=1, device_id=device(peer), device_id_type=MESH)

    lane = lax.broadcasted_iota(jnp.int32, (8, LANES), 1)
    own_id = jnp.where(lane < used, (at["z"] * 8 + plane_slot) * rows + lane // rank, -1)
    load_ids.wait()

    def count(i, total):
        for j in range(8):
            total = total + jnp.where(own_id == ids[i * 8 + j], 1.0, 0.0)
        return total

    counts = lax.fori_loop(0, val_count // 8, count, jnp.zeros((8, LANES), jnp.float32))[:1]

    left_part = jnp.zeros((32, used), jnp.float32)
    right_part = jnp.zeros((64, used), jnp.float32)
    for i in range(CHUNKS):
        for copy in loads[i]:
            copy.wait()
        part = slice(i * step, (i + 1) * step)
        left_part += dot(lp[:, part], lf[i].reshape(used, step), NT)
        right_part += dot(rp[:, part], rf[i].reshape(used, step), NT)
    own = jnp.concatenate([left_part, right_part], axis=0).astype(jnp.bfloat16)
    own = jnp.concatenate([own, jnp.zeros((96, LANES - used), jnp.bfloat16)], axis=1)
    blocks[slot] = own

    def sends(stage, buffer, index, peers):
        for peer in peers:
            pltpu.make_async_remote_copy(
                src_ref=buffer.at[index], dst_ref=buffer.at[index],
                send_sem=send_sem.at[stage], recv_sem=recv_sem.at[stage],
                device_id=device(peer), device_id_type=MESH,
            ).start()

    def all_of(stage, buffer, number):
        view = buffer.at[pl.ds(0, number)]
        return pltpu.make_async_remote_copy(
            src_ref=view, dst_ref=view, send_sem=send_sem.at[stage], recv_sem=recv_sem.at[stage],
            device_id=device(other), device_id_type=MESH,
        )

    first[at["z"]] = to_features(own[:32], own[32:], counts)
    pl.semaphore_wait(barrier, len(along_z) + len(plane) + 1)
    sends(0, first, at["z"], along_z)
    sends(1, blocks, slot, plane)
    all_of(0, first, 7).wait_recv()
    second[slot] = jnp.sum(first[...], axis=0)
    sends(2, second, slot, plane)
    all_of(1, blocks, 15).wait_recv()
    left = [jnp.concatenate([blocks[8 * l + b, :32] for b in range(8)], axis=1) for l in range(2)]
    right = [jnp.concatenate([blocks[8 * l + b, 32:] for b in range(8)], axis=1) for l in range(2)]
    all_of(2, second, 15).wait_recv()
    target = [jnp.sum(second[pl.ds(8 * l, 8)], axis=0) for l in range(2)]

    def to_examples(values, index):
        total = jnp.zeros((32, 8 * LANES), jnp.float32)
        squares = jnp.zeros((16, LANES), jnp.float32)
        for l in range(2):
            both = jnp.concatenate(split(unpack(values[l])), axis=0)
            mixed = dot(both, right[l], NN)
            total += (mixed[:32] + mixed[32:]) * left[l].astype(jnp.float32)
            squares += values[l] * values[l]
        parts = [jnp.sum(total[:, b * LANES:(b + 1) * LANES], axis=0, keepdims=True) for b in range(8)]
        mine = pair.at[index, at["c"]]
        mine[...] = jnp.concatenate(parts + [jnp.sum(squares, axis=0, keepdims=True)], axis=0)
        sends(3 + index, pair.at[index], at["c"], [other])
        all_of(3 + index, pair.at[index], 1).wait_recv()
        both = pair[index, 0] + pair[index, 1]
        each = both[:8]
        each = each + jnp.where(lane % 2 == 0, pltpu.roll(each, LANES - 1, 1), pltpu.roll(each, 1, 1))
        each = each + jnp.where(lane % 4 < 2, pltpu.roll(each, LANES - 2, 1), pltpu.roll(each, 2, 1))
        return each, jnp.sum(both[8:9], axis=1, keepdims=True)

    def to_all_features(vector, index, extra):
        row = jnp.concatenate([vector[b:b + 1] for b in range(8)], axis=1)
        parts = [to_features(left[l], right[l], row) for l in range(2)]
        parts += [jnp.sum(e, axis=0, keepdims=True) for e in extra]
        sums[index, at["z"]] = jnp.concatenate(parts, axis=0)
        sends(6 + index, sums.at[index], at["z"], along_z)
        all_of(6 + index, sums.at[index], 7).wait_recv()
        whole = jnp.sum(sums[index], axis=0)
        scalars = [jnp.sum(whole[32 + i:33 + i], axis=1, keepdims=True) * (1.0 / rank) for i in range(2)]
        return [whole[:16], whole[16:32]], scalars

    scale = 1.0 / (rank * total_features)
    align, _ = to_examples(target, 0)
    residual = align * (math.sqrt(val_count / total_features) / (val_count * rank))
    start = residual
    mixed, (norm, _) = to_all_features(residual, 0, [residual * residual, jnp.zeros_like(residual)])
    image, square = to_examples(mixed, 1)
    image = image * scale + RIDGE * start
    alpha = norm / (square * scale + RIDGE * norm)
    weights = alpha * start
    residual = start - alpha * image
    again, (norm_next, cross) = to_all_features(residual, 1, [residual * residual, residual * start])
    beta = norm_next / norm
    direction = residual + beta * start
    mixed = [again[l] + beta * mixed[l] for l in range(2)]
    image, square = to_examples(mixed, 2)
    image = image * scale + RIDGE * direction
    length = norm_next + 2.0 * beta * cross + beta * beta * norm
    alpha = norm_next / (square * scale + RIDGE * length)
    weights = weights + alpha * direction
    residual = residual - alpha * image

    mine = lax.broadcasted_iota(jnp.int32, (8, LANES), 0) == plane_slot
    pieces = []
    for value in (weights, residual):
        value = jnp.sum(jnp.where(mine, value, 0.0), axis=0, keepdims=True)
        for _ in range(3):
            high = value.astype(jnp.bfloat16)
            pieces.append(high.astype(jnp.float32))
            value = value - high.astype(jnp.float32)
    pieces.append(jnp.zeros((2, LANES), jnp.float32))
    take = (
        lax.broadcasted_iota(jnp.int32, (LANES, LANES), 0)
        == rank * lax.broadcasted_iota(jnp.int32, (LANES, LANES), 1)
    )
    taken = dot(
        jnp.concatenate(pieces, axis=0).astype(jnp.bfloat16),
        jnp.where(take, 1.0, 0.0).astype(jnp.bfloat16), NN,
    )
    out_ref[0:1] = taken[0:1] + taken[1:2] + taken[2:3]
    out_ref[1:2] = taken[3:4] + taken[4:5] + taken[5:6]

    all_of(0, first, 7).wait_send()
    all_of(1, blocks, 15).wait_send()
    all_of(2, second, 15).wait_send()
    for i in range(3):
        all_of(3 + i, pair.at[i], 1).wait_send()
    for i in range(2):
        all_of(6 + i, sums.at[i], 7).wait_send()


def per_device(left_factors, right_factors, left_proj, right_proj, val_ids):
    _, rows, rank, width = left_factors.shape
    left_proj = jnp.swapaxes(left_proj, 1, 2)
    right_proj = jnp.swapaxes(right_proj, 1, 2)
    ka, kb = left_proj.shape[1], right_proj.shape[1]
    val_count = val_ids.shape[0]
    total_features = ka * kb * lax.axis_size("feat")
    step = width // CHUNKS
    out = pl.pallas_call(
        functools.partial(kernel, rows, rank, total_features, val_count),
        out_shape=jax.ShapeDtypeStruct((2, LANES), jnp.float32),
        in_specs=[pl.BlockSpec(memory_space=pltpu.HBM)] * 5,
        out_specs=pl.BlockSpec(memory_space=pltpu.VMEM),
        scratch_shapes=[
            pltpu.VMEM((CHUNKS, rows, rank, step), jnp.bfloat16),
            pltpu.VMEM((CHUNKS, rows, rank, step), jnp.bfloat16),
            pltpu.VMEM((ka, width), jnp.bfloat16),
            pltpu.VMEM((kb, width), jnp.bfloat16),
            pltpu.SMEM((val_count,), jnp.int32),
            pltpu.VMEM((16, ka + kb, LANES), jnp.bfloat16),
            pltpu.VMEM((8, 16, LANES), jnp.float32),
            pltpu.VMEM((16, 16, LANES), jnp.float32),
            pltpu.VMEM((2, 8, 34, LANES), jnp.float32),
            pltpu.VMEM((3, 2, 9, LANES), jnp.float32),
            pltpu.SemaphoreType.DMA((CHUNKS, 4)),
            pltpu.SemaphoreType.DMA,
            pltpu.SemaphoreType.DMA((8,)),
            pltpu.SemaphoreType.DMA((8,)),
        ],
        compiler_params=pltpu.CompilerParams(
            collective_id=0, has_side_effects=True, vmem_limit_bytes=56 * 2**20
        ),
        name="reweight",
    )(left_factors, right_factors, left_proj, right_proj, val_ids)
    return out[0, :rows], out[1, :rows]


def solution(mesh):
    return jax.shard_map(
        per_device,
        mesh=mesh,
        in_specs=(
            P("feat", "ex", None, None),
            P("feat", "ex", None, None),
            P("feat", None, None),
            P("feat", None, None),
            P(),
        ),
        out_specs=(P("ex"), P("ex")),
        check_vma=False,
    )
```

```python
import functools
import math

import jax
import jax.numpy as jnp
from jax import lax
from jax.experimental import pallas as pl
from jax.experimental.pallas import tpu as pltpu
from jax.sharding import PartitionSpec as P

MESH = pl.DeviceIdType.MESH
NT = (((1,), (1,)), ((), ()))
NN = (((1,), (0,)), ((), ()))
SIZE = dict(z=8, y=4, xh=2, xl=2, c=2)
RIDGE = 0.5
CHUNKS = 4
LANES = 128
GROUP = 32


def coordinates():
    ex = lax.axis_index("ex")
    feat = lax.axis_index("feat")
    return dict(z=ex // 8, y=(ex // 2) % 4, xh=ex % 2, xl=feat // 2, c=feat % 2)


def device(at):
    return (at["z"] * 8 + at["y"] * 2 + at["xh"], at["xl"] * 2 + at["c"])


def moved(at, **steps):
    new = dict(at)
    for axis, step in steps.items():
        if not (isinstance(step, int) and step == 0):
            new[axis] = (at[axis] + step) % SIZE[axis]
    return new


def hops(y, xh, xl):
    x = 2 * xh + xl
    return min(y, 4 - y) + min(x, 4 - x)


def split(value):
    high = value.astype(jnp.bfloat16)
    low = (value - high.astype(jnp.float32)).astype(jnp.bfloat16)
    return jnp.concatenate([high, low], axis=0)


def pack(value):
    return jnp.concatenate([value[:16], value[16:]], axis=1)


def unpack(value):
    return jnp.concatenate([value[:, :64], value[:, 64:]], axis=0)


def dot(a, b, dims):
    return lax.dot_general(a, b, dims, preferred_element_type=jnp.float32)


def to_features(left, right, row):
    sums = dot(split(left.astype(jnp.float32) * row), right, NT)
    return pack(sums[:32] + sums[32:])


def to_lanes(left, right, values):
    total = None
    for l in range(2):
        mixed = dot(split(unpack(values[l])), right[l], NN)
        term = (mixed[:32] + mixed[32:]) * left[l].astype(jnp.float32)
        total = term if total is None else total + term
    return jnp.sum(total, axis=0, keepdims=True)


def rows_of(line):
    return jnp.concatenate([line[:, i:i + LANES] for i in range(0, line.shape[1], LANES)], axis=0)


def line_of(rows):
    return jnp.concatenate([rows[i:i + 1] for i in range(rows.shape[0])], axis=1)


def over_rank(rows):
    rows = rows + pltpu.roll(rows, 2 * GROUP, 1)
    return rows + pltpu.roll(rows, GROUP, 1)


def total(row):
    return jnp.sum(row, axis=1, keepdims=True)


def squares(values):
    return jnp.sum(values[0] * values[0] + values[1] * values[1], axis=0, keepdims=True)


def kernel(
    rows, rank, total_features, val_count,
    lf_hbm, rf_hbm, lp_hbm, rp_hbm, ids_hbm, out_ref,
    lf, rf, lp, rp, ids, blocks, first, second, sums, last, pair_0, pair_1, pair_2, pair_3,
    load_sem, ids_sem, send_sem, recv_sem,
):
    at = coordinates()
    width = lf_hbm.shape[3]
    step = width // CHUNKS
    used = rows * rank
    plane_slot = at["y"] * 2 + at["xh"]
    slot = at["xl"] * 8 + plane_slot
    two = at["z"] // 2
    sign = 2 * (at["z"] % 2) - 1

    along_z = [moved(at, z=d) for d in (4, 3, 5, 2, 6, 1, 7)]
    next_twos = [moved(at, z=sign * d + 8) for d in (3, 2, 1)]
    twin = moved(at, z=8 - sign)
    plane = [(y, xh, xl) for y in range(4) for xh in range(2) for xl in range(2) if y or xh or xl]
    plane = [moved(at, y=y, xh=xh, xl=xl) for y, xh, xl in sorted(plane, key=lambda o: -hops(*o))]
    other = moved(at, c=1)
    barrier = pltpu.get_barrier_semaphore()
    for peer in along_z + plane + [other]:
        pl.semaphore_signal(barrier, inc=1, device_id=device(peer), device_id_type=MESH)

    loads = []
    for i in range(CHUNKS):
        part = pl.ds(i * step, step)
        group = [
            pltpu.make_async_copy(lp_hbm.at[0, :, part], lp.at[:, part], load_sem.at[i, 0]),
            pltpu.make_async_copy(lf_hbm.at[0, :, :, part], lf.at[i], load_sem.at[i, 1]),
            pltpu.make_async_copy(rp_hbm.at[0, :, part], rp.at[:, part], load_sem.at[i, 2]),
            pltpu.make_async_copy(rf_hbm.at[0, :, :, part], rf.at[i], load_sem.at[i, 3]),
        ]
        for copy in group:
            copy.start()
        loads.append(group)
    load_ids = pltpu.make_async_copy(ids_hbm, ids, ids_sem)
    load_ids.start()

    lane = lax.broadcasted_iota(jnp.int32, (8, LANES), 1) % GROUP
    own_id = jnp.where(lane < rows, (at["z"] * 8 + plane_slot) * rows + lane, -1)
    load_ids.wait()

    def count(i, counts):
        for j in range(8):
            counts = counts + jnp.where(own_id == ids[i * 8 + j], 1.0, 0.0)
        return counts

    counts = lax.fori_loop(0, val_count // 8, count, jnp.zeros((8, LANES), jnp.float32))[:1]

    left_part = jnp.zeros((32, used), jnp.float32)
    right_part = jnp.zeros((64, used), jnp.float32)
    for i in range(CHUNKS):
        for copy in loads[i]:
            copy.wait()
        part = slice(i * step, (i + 1) * step)
        left_part += dot(lp[:, part], lf[i].reshape(used, step), NT)
        right_part += dot(rp[:, part], rf[i].reshape(used, step), NT)
    own = jnp.concatenate([left_part, right_part], axis=0).astype(jnp.bfloat16)
    source = lax.broadcasted_iota(jnp.int32, (used, LANES), 0)
    goal = lax.broadcasted_iota(jnp.int32, (used, LANES), 1)
    order = jnp.where((source // rank == goal % GROUP) & (source % rank == goal // GROUP), 1.0, 0.0)
    own = dot(own, order.astype(jnp.bfloat16), NN).astype(jnp.bfloat16)
    blocks[slot] = own

    def send(stage, source, goal, peers):
        for peer in peers:
            pltpu.make_async_remote_copy(
                src_ref=source, dst_ref=goal, send_sem=send_sem.at[stage], recv_sem=recv_sem.at[stage],
                device_id=device(peer), device_id_type=MESH,
            ).start()

    def all_of(stage, view):
        return pltpu.make_async_remote_copy(
            src_ref=view, dst_ref=view, send_sem=send_sem.at[stage], recv_sem=recv_sem.at[stage],
            device_id=device(other), device_id_type=MESH,
        )

    def share(stage, buffer, index, value, peers):
        buffer[index] = value
        send(stage, buffer.at[index], buffer.at[index], peers)

    def factors(base):
        left = [jnp.concatenate([blocks[base + 8 * l + b, :32] for b in range(8)], axis=1) for l in range(2)]
        right = [jnp.concatenate([blocks[base + 8 * l + b, 32:] for b in range(8)], axis=1) for l in range(2)]
        return left, right

    target = to_features(own[:32], own[32:], counts)
    pl.semaphore_wait(barrier, len(along_z) + len(plane) + 1)
    share(0, first, at["z"], target, along_z)
    send(1, blocks.at[slot], blocks.at[slot], plane)
    send(3, blocks.at[slot], blocks.at[16 + slot], [twin])
    all_of(0, first.at[pl.ds(0, 7)]).wait_recv()
    share(2, second, slot, jnp.sum(first[...], axis=0), plane)
    all_of(3, blocks.at[16 + slot]).wait_recv()
    send(4, blocks.at[16 + slot], blocks.at[16 + slot], plane)
    all_of(1, blocks.at[pl.ds(0, 15)]).wait_recv()
    all_of(2, second.at[pl.ds(0, 15)]).wait_recv()
    target = [jnp.sum(second[pl.ds(8 * l, 8)], axis=0) for l in range(2)]

    scale = 1.0 / (rank * total_features)
    align_scale = math.sqrt(val_count / total_features) / (val_count * rank)

    share(5, pair_0, at["c"], rows_of(to_lanes(*factors(0), target)), [other])
    all_of(5, pair_0.at[0]).wait_recv()
    start = over_rank(pair_0[0] + pair_0[1]) * align_scale

    left, right = factors(0)
    line = line_of(start)
    norm_row = jnp.sum(start * start, axis=0, keepdims=True)
    value = jnp.concatenate([to_features(left[l], right[l], line) for l in range(2)] + [norm_row], axis=0)
    share(9, sums, at["z"], value, along_z)

    all_of(4, blocks.at[pl.ds(16, 15)]).wait_recv()
    share(6, pair_1, at["c"], rows_of(to_lanes(*factors(16), target)), [other])
    all_of(6, pair_1.at[0]).wait_recv()
    twin_start = over_rank(pair_1[0] + pair_1[1]) * align_scale

    all_of(9, sums.at[pl.ds(0, 7)]).wait_recv()
    whole = jnp.sum(sums[...], axis=0)
    mixed = [whole[:16], whole[16:32]]
    norm = total(whole[32:33]) * (1.0 / rank)
    value = [rows_of(to_lanes(*factors(0), mixed)), rows_of(to_lanes(*factors(16), mixed)), squares(mixed)]
    share(7, pair_2, at["c"], jnp.concatenate(value, axis=0), [other])
    all_of(7, pair_2.at[0]).wait_recv()
    both = pair_2[0] + pair_2[1]
    product = over_rank(both[:16])
    alpha = norm / (total(both[16:17]) * scale + RIDGE * norm)
    start = jnp.concatenate([start, twin_start], axis=0)
    residual = start - alpha * (product * scale + RIDGE * start)

    line = line_of(residual)
    value = []
    for l in range(2):
        value.append(to_features(
            jnp.concatenate([factors(0)[0][l], factors(16)[0][l]], axis=1),
            jnp.concatenate([factors(0)[1][l], factors(16)[1][l]], axis=1),
            line,
        ))
    value.append(jnp.sum(residual * residual, axis=0, keepdims=True))
    value.append(jnp.sum(residual * start, axis=0, keepdims=True))
    share(10, last, two, jnp.concatenate(value, axis=0), next_twos)

    mine = lax.broadcasted_iota(jnp.int32, (16, LANES), 0) == plane_slot

    def own_row(value):
        return jnp.sum(jnp.where(mine, value, 0.0), axis=0, keepdims=True)

    start, residual, product = own_row(start), own_row(residual), own_row(product)
    weights = alpha * start
    left = [blocks[8 * l + plane_slot, :32] for l in range(2)]
    right = [blocks[8 * l + plane_slot, 32:] for l in range(2)]

    all_of(10, last.at[pl.ds(0, 3)]).wait_recv()
    whole = jnp.sum(last[...], axis=0)
    again = [whole[:16], whole[16:32]]
    norm_next = total(whole[32:33]) * (1.0 / rank)
    cross = total(whole[33:34]) * (1.0 / rank)
    beta = norm_next / norm
    again_row = to_lanes(left, right, again)
    square = squares([again[l] + beta * mixed[l] for l in range(2)])
    share(8, pair_3, at["c"], jnp.concatenate([again_row, square], axis=0), [other])
    direction = residual + beta * start
    length = norm_next + 2.0 * beta * cross + beta * beta * norm
    all_of(8, pair_3.at[0]).wait_recv()
    both = pair_3[0] + pair_3[1]
    product = over_rank(both)[:1] + beta * product
    image = product * scale + RIDGE * direction
    alpha = norm_next / (total(both[1:2]) * scale + RIDGE * length)
    out_ref[0:1] = weights + alpha * direction
    out_ref[1:2] = residual - alpha * image

    all_of(0, first.at[pl.ds(0, 7)]).wait_send()
    all_of(1, blocks.at[pl.ds(0, 15)]).wait_send()
    all_of(2, second.at[pl.ds(0, 15)]).wait_send()
    all_of(3, blocks.at[0]).wait_send()
    all_of(4, blocks.at[pl.ds(0, 15)]).wait_send()
    all_of(5, pair_0.at[0]).wait_send()
    all_of(6, pair_1.at[0]).wait_send()
    all_of(7, pair_2.at[0]).wait_send()
    all_of(8, pair_3.at[0]).wait_send()
    all_of(9, sums.at[pl.ds(0, 7)]).wait_send()
    all_of(10, last.at[pl.ds(0, 3)]).wait_send()


def per_device(left_factors, right_factors, left_proj, right_proj, val_ids):
    _, rows, rank, width = left_factors.shape
    left_proj = jnp.swapaxes(left_proj, 1, 2)
    right_proj = jnp.swapaxes(right_proj, 1, 2)
    ka, kb = left_proj.shape[1], right_proj.shape[1]
    val_count = val_ids.shape[0]
    total_features = ka * kb * lax.axis_size("feat")
    step = width // CHUNKS
    operands = (left_factors, right_factors, left_proj, right_proj, val_ids)
    out = pl.pallas_call(
        functools.partial(kernel, rows, rank, total_features, val_count),
        out_shape=jax.ShapeDtypeStruct((2, LANES), jnp.float32),
        in_specs=[pl.BlockSpec(memory_space=pltpu.HBM)] * 5,
        out_specs=pl.BlockSpec(memory_space=pltpu.VMEM),
        scratch_shapes=[
            pltpu.VMEM((CHUNKS, rows, rank, step), jnp.bfloat16),
            pltpu.VMEM((CHUNKS, rows, rank, step), jnp.bfloat16),
            pltpu.VMEM((ka, width), jnp.bfloat16),
            pltpu.VMEM((kb, width), jnp.bfloat16),
            pltpu.SMEM((val_count,), jnp.int32),
            pltpu.VMEM((32, ka + kb, LANES), jnp.bfloat16),
            pltpu.VMEM((8, 16, LANES), jnp.float32),
            pltpu.VMEM((16, 16, LANES), jnp.float32),
            pltpu.VMEM((8, 33, LANES), jnp.float32),
            pltpu.VMEM((4, 34, LANES), jnp.float32),
            pltpu.VMEM((2, 8, LANES), jnp.float32),
            pltpu.VMEM((2, 8, LANES), jnp.float32),
            pltpu.VMEM((2, 17, LANES), jnp.float32),
            pltpu.VMEM((2, 2, LANES), jnp.float32),
            pltpu.SemaphoreType.DMA((CHUNKS, 4)),
            pltpu.SemaphoreType.DMA,
            pltpu.SemaphoreType.DMA((11,)),
            pltpu.SemaphoreType.DMA((11,)),
        ],
        compiler_params=pltpu.CompilerParams(
            collective_id=0, has_side_effects=True, vmem_limit_bytes=32 * 2**20
        ),
        name="reweight",
    )(*(pltpu.with_memory_space_constraint(a, pltpu.HBM) for a in operands))
    return out[0, :rows], out[1, :rows]


def solution(mesh):
    return jax.shard_map(
        per_device,
        mesh=mesh,
        in_specs=(
            P("feat", "ex", None, None),
            P("feat", "ex", None, None),
            P("feat", None, None),
            P("feat", None, None),
            P(),
        ),
        out_specs=(P("ex"), P("ex")),
        check_vma=False,
    )
```

```python
import functools
import math

import jax
import jax.numpy as jnp
from jax import lax
from jax.experimental import pallas as pl
from jax.experimental.pallas import tpu as pltpu
from jax.sharding import PartitionSpec as P

MESH = pl.DeviceIdType.MESH
NT = (((1,), (1,)), ((), ()))
NN = (((1,), (0,)), ((), ()))
SIZE = dict(z=8, y=4, xh=2, xl=2, c=2)
RIDGE = 0.5
CHUNKS = 2
LANES = 128
GROUP = 32


def coordinates():
    ex = lax.axis_index("ex")
    feat = lax.axis_index("feat")
    return dict(z=ex // 8, y=(ex // 2) % 4, xh=ex % 2, xl=feat // 2, c=feat % 2)


def device(at):
    return (at["z"] * 8 + at["y"] * 2 + at["xh"], at["xl"] * 2 + at["c"])


def moved(at, **steps):
    new = dict(at)
    for axis, step in steps.items():
        if step:
            new[axis] = (at[axis] + step) % SIZE[axis]
    return new


def hops(y, xh, xl):
    x = 2 * xh + xl
    return min(y, 4 - y) + min(x, 4 - x)


def split(value):
    high = value.astype(jnp.bfloat16)
    low = (value - high.astype(jnp.float32)).astype(jnp.bfloat16)
    return jnp.concatenate([high, low], axis=0)


def pack(value):
    return jnp.concatenate([value[:16], value[16:]], axis=1)


def unpack(value):
    return jnp.concatenate([value[:, :64], value[:, 64:]], axis=0)


def dot(a, b, dims):
    return lax.dot_general(a, b, dims, preferred_element_type=jnp.float32)


def to_features(left, right, row):
    sums = dot(split(left.astype(jnp.float32) * row), right, NT)
    return pack(sums[:32] + sums[32:])


def to_lanes(left, right, values):
    total = None
    for l in range(2):
        mixed = dot(split(unpack(values[l])), right[l], NN)
        term = (mixed[:32] + mixed[32:]) * left[l].astype(jnp.float32)
        total = term if total is None else total + term
    return jnp.sum(total, axis=0, keepdims=True)


def rows_of(line):
    return jnp.concatenate([line[:, i:i + LANES] for i in range(0, line.shape[1], LANES)], axis=0)


def line_of(rows):
    return jnp.concatenate([rows[i:i + 1] for i in range(rows.shape[0])], axis=1)


def over_rank(rows):
    rows = rows + pltpu.roll(rows, 2 * GROUP, 1)
    return rows + pltpu.roll(rows, GROUP, 1)


def total(row):
    return jnp.sum(row, axis=1, keepdims=True)


def thirds(value):
    parts = []
    for _ in range(3):
        parts.append(value.astype(jnp.bfloat16).astype(jnp.float32))
        value = value - parts[-1]
    return parts + [jnp.zeros((10, LANES), jnp.float32)]


def squares(values):
    return jnp.sum(values[0] * values[0] + values[1] * values[1], axis=0, keepdims=True)


def kernel(
    rows, rank, total_features, val_count,
    lf_hbm, rf_hbm, lp_hbm, rp_hbm, ids_hbm, out_ref,
    lf, rf, lp, rp, ids, blocks, first, second, sums, pair_0, pair_1, pair_2,
    load_sem, ids_sem, send_sem, recv_sem,
):
    at = coordinates()
    width = lf_hbm.shape[3]
    step = width // CHUNKS
    used = rows * rank
    plane_slot = at["y"] * 2 + at["xh"]
    slot = at["xl"] * 8 + plane_slot

    along_z = [moved(at, z=d) for d in (4, 3, 5, 2, 6, 1, 7)]
    plane = [(y, xh, xl) for y in range(4) for xh in range(2) for xl in range(2) if y or xh or xl]
    plane = [moved(at, y=y, xh=xh, xl=xl) for y, xh, xl in sorted(plane, key=lambda o: -hops(*o))]
    other = moved(at, c=1)
    barrier = pltpu.get_barrier_semaphore()
    order = along_z[:1] + plane[:1] + along_z[1:3] + plane[1:5]
    rest = along_z[3:] + plane[5:] + [other]

    def greet(peers):
        for peer in peers:
            pl.semaphore_signal(barrier, inc=1, device_id=device(peer), device_id_type=MESH)

    greet(order)

    loads = []
    for i in range(CHUNKS):
        part = pl.ds(i * step, step)
        group = [
            pltpu.make_async_copy(lp_hbm.at[0, :, part], lp.at[:, part], load_sem.at[i, 0]),
            pltpu.make_async_copy(lf_hbm.at[0, :, :, part], lf.at[i], load_sem.at[i, 1]),
            pltpu.make_async_copy(rp_hbm.at[0, :, part], rp.at[:, part], load_sem.at[i, 2]),
            pltpu.make_async_copy(rf_hbm.at[0, :, :, part], rf.at[i], load_sem.at[i, 3]),
        ]
        for copy in group:
            copy.start()
        loads.append(group)
    load_ids = pltpu.make_async_copy(ids_hbm, ids, ids_sem)
    load_ids.start()
    greet(rest)

    lane = lax.broadcasted_iota(jnp.int32, (8, LANES), 1) % GROUP
    own_id = jnp.where(lane < rows, (at["z"] * 8 + plane_slot) * rows + lane, -1)
    load_ids.wait()

    def count(i, counts):
        for j in range(8):
            counts = counts + jnp.where(own_id == ids[i * 8 + j], 1.0, 0.0)
        return counts

    counts = lax.fori_loop(0, val_count // 8, count, jnp.zeros((8, LANES), jnp.float32))[:1]

    left_part = jnp.zeros((32, used), jnp.float32)
    right_part = jnp.zeros((64, used), jnp.float32)
    for i in range(CHUNKS):
        for copy in loads[i]:
            copy.wait()
        part = slice(i * step, (i + 1) * step)
        left_part += dot(lp[:, part], lf[i].reshape(used, step), NT)
        right_part += dot(rp[:, part], rf[i].reshape(used, step), NT)
    own = jnp.concatenate([left_part, right_part], axis=0).astype(jnp.bfloat16)
    source = lax.broadcasted_iota(jnp.int32, (used, LANES), 0)
    goal = lax.broadcasted_iota(jnp.int32, (used, LANES), 1)
    place = jnp.where((source // rank == goal % GROUP) & (source % rank == goal // GROUP), 1.0, 0.0)
    own = dot(own, place.astype(jnp.bfloat16), NN).astype(jnp.bfloat16)
    blocks[slot] = own

    def send(stage, source, goal, peers):
        for peer in peers:
            pltpu.make_async_remote_copy(
                src_ref=source, dst_ref=goal, send_sem=send_sem.at[stage], recv_sem=recv_sem.at[stage],
                device_id=device(peer), device_id_type=MESH,
            ).start()

    def all_of(stage, view):
        return pltpu.make_async_remote_copy(
            src_ref=view, dst_ref=view, send_sem=send_sem.at[stage], recv_sem=recv_sem.at[stage],
            device_id=device(other), device_id_type=MESH,
        )

    def share(stage, buffer, index, value, peers):
        buffer[index] = value
        send(stage, buffer.at[index], buffer.at[index], peers)

    target = to_features(own[:32], own[32:], counts)
    pl.semaphore_wait(barrier, len(along_z) + len(plane) + 1)
    share(0, first, at["z"], target.astype(first.dtype), along_z)
    send(1, blocks.at[slot], blocks.at[slot], plane)
    all_of(0, first.at[pl.ds(0, 7)]).wait_recv()
    share(2, second, slot, jnp.sum(first[...].astype(jnp.float32), axis=0).astype(second.dtype), plane)
    all_of(1, blocks.at[pl.ds(0, 15)]).wait_recv()
    all_of(2, second.at[pl.ds(0, 15)]).wait_recv()
    target = [jnp.sum(second[pl.ds(8 * l, 8)].astype(jnp.float32), axis=0) for l in range(2)]
    left = [jnp.concatenate([blocks[8 * l + b, :32] for b in range(8)], axis=1) for l in range(2)]
    right = [jnp.concatenate([blocks[8 * l + b, 32:] for b in range(8)], axis=1) for l in range(2)]

    def send_features(index, rows, scalars):
        line = line_of(rows)
        value = [to_features(left[l], right[l], line) for l in range(2)]
        value += thirds(jnp.concatenate([jnp.sum(s, axis=0, keepdims=True) for s in scalars], axis=0))
        value = jnp.concatenate(value, axis=0).astype(jnp.bfloat16)
        share(6 + index, sums.at[index], at["z"], value, along_z)

    def take_features(index):
        all_of(6 + index, sums.at[index, pl.ds(0, 7)]).wait_recv()
        whole = jnp.sum(sums[index].astype(jnp.float32), axis=0)
        scalars = total(whole[32:40] + whole[40:48]) * (1.0 / rank)
        return [whole[:16], whole[16:32]], scalars[0:1] + scalars[2:3] + scalars[4:5], scalars[1:2] + scalars[3:4] + scalars[5:6]

    scale = 1.0 / (rank * total_features)
    align_scale = math.sqrt(val_count / total_features) / (val_count * rank)

    share(3, pair_0, at["c"], rows_of(to_lanes(left, right, target)), [other])
    all_of(3, pair_0.at[0]).wait_recv()
    start = over_rank(pair_0[0] + pair_0[1]) * align_scale
    send_features(0, start, [start * start, start])
    mixed, norm, _ = take_features(0)

    value = jnp.concatenate([rows_of(to_lanes(left, right, mixed)), squares(mixed)], axis=0)
    share(4, pair_1, at["c"], value, [other])
    all_of(4, pair_1.at[0]).wait_recv()
    both = pair_1[0] + pair_1[1]
    product = over_rank(both[:8])
    alpha = norm / (total(both[8:9]) * scale + RIDGE * norm)
    residual = start - alpha * (product * scale + RIDGE * start)
    send_features(1, residual, [residual * residual, residual * start])

    mine = lax.broadcasted_iota(jnp.int32, (8, LANES), 0) == plane_slot

    def own_row(value):
        return jnp.sum(jnp.where(mine, value, 0.0), axis=0, keepdims=True)

    start, residual, product = own_row(start), own_row(residual), own_row(product)
    weights = alpha * start
    left = [blocks[8 * l + plane_slot, :32] for l in range(2)]
    right = [blocks[8 * l + plane_slot, 32:] for l in range(2)]

    again, norm_next, cross = take_features(1)
    beta = norm_next / norm
    again_row = to_lanes(left, right, again)
    square = squares([again[l] + beta * mixed[l] for l in range(2)])
    share(5, pair_2, at["c"], jnp.concatenate([again_row, square], axis=0), [other])
    direction = residual + beta * start
    length = norm_next + 2.0 * beta * cross + beta * beta * norm
    all_of(5, pair_2.at[0]).wait_recv()
    both = pair_2[0] + pair_2[1]
    product = over_rank(both)[:1] + beta * product
    image = product * scale + RIDGE * direction
    alpha = norm_next / (total(both[1:2]) * scale + RIDGE * length)
    out_ref[0:1] = weights + alpha * direction
    out_ref[1:2] = residual - alpha * image

    all_of(0, first.at[pl.ds(0, 7)]).wait_send()
    all_of(1, blocks.at[pl.ds(0, 15)]).wait_send()
    all_of(2, second.at[pl.ds(0, 15)]).wait_send()
    for i, pair in enumerate((pair_0, pair_1, pair_2)):
        all_of(3 + i, pair.at[0]).wait_send()
    for i in range(2):
        all_of(6 + i, sums.at[i, pl.ds(0, 7)]).wait_send()


def per_device(left_factors, right_factors, left_proj, right_proj, val_ids):
    _, rows, rank, width = left_factors.shape
    left_proj = jnp.swapaxes(left_proj, 1, 2)
    right_proj = jnp.swapaxes(right_proj, 1, 2)
    ka, kb = left_proj.shape[1], right_proj.shape[1]
    val_count = val_ids.shape[0]
    total_features = ka * kb * lax.axis_size("feat")
    step = width // CHUNKS
    operands = (left_factors, right_factors, left_proj, right_proj, val_ids)
    out = pl.pallas_call(
        functools.partial(kernel, rows, rank, total_features, val_count),
        out_shape=jax.ShapeDtypeStruct((2, LANES), jnp.float32),
        in_specs=[pl.BlockSpec(memory_space=pltpu.HBM)] * 5,
        out_specs=pl.BlockSpec(memory_space=pltpu.VMEM),
        scratch_shapes=[
            pltpu.VMEM((CHUNKS, rows, rank, step), jnp.bfloat16),
            pltpu.VMEM((CHUNKS, rows, rank, step), jnp.bfloat16),
            pltpu.VMEM((ka, width), jnp.bfloat16),
            pltpu.VMEM((kb, width), jnp.bfloat16),
            pltpu.SMEM((val_count,), jnp.int32),
            pltpu.VMEM((16, ka + kb, LANES), jnp.bfloat16),
            pltpu.VMEM((8, 16, LANES), jnp.bfloat16),
            pltpu.VMEM((16, 16, LANES), jnp.bfloat16),
            pltpu.VMEM((2, 8, 48, LANES), jnp.bfloat16),
            pltpu.VMEM((2, 8, LANES), jnp.float32),
            pltpu.VMEM((2, 9, LANES), jnp.float32),
            pltpu.VMEM((2, 2, LANES), jnp.float32),
            pltpu.SemaphoreType.DMA((CHUNKS, 4)),
            pltpu.SemaphoreType.DMA,
            pltpu.SemaphoreType.DMA((8,)),
            pltpu.SemaphoreType.DMA((8,)),
        ],
        compiler_params=pltpu.CompilerParams(
            collective_id=0, has_side_effects=True, vmem_limit_bytes=32 * 2**20
        ),
        name="reweight",
    )(*(pltpu.with_memory_space_constraint(a, pltpu.HBM) for a in operands))
    return out[0, :rows], out[1, :rows]


def solution(mesh):
    return jax.shard_map(
        per_device,
        mesh=mesh,
        in_specs=(
            P("feat", "ex", None, None),
            P("feat", "ex", None, None),
            P("feat", None, None),
            P("feat", None, None),
            P(),
        ),
        out_specs=(P("ex"), P("ex")),
        check_vma=False,
    )
```

```python
import functools
import math

import jax
import jax.numpy as jnp
from jax import lax
from jax.experimental import pallas as pl
from jax.experimental.pallas import tpu as pltpu
from jax.sharding import PartitionSpec as P

MESH = pl.DeviceIdType.MESH
NT = (((1,), (1,)), ((), ()))
NN = (((1,), (0,)), ((), ()))
SIZE = dict(z=8, y=4, xh=2, xl=2, c=2)
RIDGE = 0.5
CHUNKS = 2
LANES = 128
GROUP = 32


def coordinates():
    ex = lax.axis_index("ex")
    feat = lax.axis_index("feat")
    return dict(z=ex // 8, y=(ex // 2) % 4, xh=ex % 2, xl=feat // 2, c=feat % 2)


def device(at):
    return (at["z"] * 8 + at["y"] * 2 + at["xh"], at["xl"] * 2 + at["c"])


def moved(at, **steps):
    new = dict(at)
    for axis, step in steps.items():
        if step:
            new[axis] = (at[axis] + step) % SIZE[axis]
    return new


def hops(y, xh, xl):
    x = 2 * xh + xl
    return min(y, 4 - y) + min(x, 4 - x)


def split(value):
    high = value.astype(jnp.bfloat16)
    low = (value - high.astype(jnp.float32)).astype(jnp.bfloat16)
    return jnp.concatenate([high, low], axis=0)


def pack(value):
    return jnp.concatenate([value[:16], value[16:]], axis=1)


def unpack(value):
    return jnp.concatenate([value[:, :64], value[:, 64:]], axis=0)


def dot(a, b, dims):
    return lax.dot_general(a, b, dims, preferred_element_type=jnp.float32)


def to_features(left, right, row):
    sums = dot(split(left.astype(jnp.float32) * row), right, NT)
    return pack(sums[:32] + sums[32:])


def to_lanes(left, right, values, ranks=lambda term: term):
    total = None
    for l in range(2):
        mixed = dot(split(unpack(values[l])), right[l], NN)
        term = ranks((mixed[:32] + mixed[32:]) * left[l].astype(jnp.float32))
        total = term if total is None else total + term
    return jnp.sum(total, axis=0, keepdims=True)


def over_rank(rows):
    rows = rows + pltpu.roll(rows, 2 * GROUP, 1)
    return rows + pltpu.roll(rows, GROUP, 1)


def total(row):
    return jnp.sum(row, axis=1, keepdims=True)


def products(a, b):
    return jnp.sum(a[0] * b[0] + a[1] * b[1], axis=0, keepdims=True)


def halves(line):
    return line[:, :LANES] + line[:, LANES:]


def ranks_added(line):
    n = line.shape[1] // 4
    return (line[:, :n] + line[:, n:2 * n]) + (line[:, 2 * n:3 * n] + line[:, 3 * n:])


def kernel(
    rows, rank, total_features, val_count,
    lf_hbm, rf_hbm, lp_hbm, rp_hbm, ids_hbm, out_ref,
    lf, rf, lp, rp, ids, blocks, wide, first, second, sums, norms, pair_0, pair_1, pair_2,
    load_sem, ids_sem, send_sem, recv_sem,
):
    at = coordinates()
    width = lf_hbm.shape[3]
    step = width // CHUNKS
    used = rows * rank
    plane_slot = at["y"] * 2 + at["xh"]
    slot = at["xl"] * 8 + plane_slot

    along_z = [moved(at, z=d) for d in (4, 3, 5, 2, 6, 1, 7)]
    plane = [(y, xh, xl) for y in range(4) for xh in range(2) for xl in range(2) if y or xh or xl]
    plane = [moved(at, y=y, xh=xh, xl=xl) for y, xh, xl in sorted(plane, key=lambda o: -hops(*o))]
    other = moved(at, c=1)
    barrier = pltpu.get_barrier_semaphore()
    order = along_z[:1] + plane[:1] + along_z[1:3] + plane[1:5]
    rest = along_z[3:] + plane[5:] + [other]

    def greet(peers):
        for peer in peers:
            pl.semaphore_signal(barrier, inc=1, device_id=device(peer), device_id_type=MESH)

    greet(order)

    loads = []
    for i in range(CHUNKS):
        part = pl.ds(i * step, step)
        group = [
            pltpu.make_async_copy(lp_hbm.at[0, :, part], lp.at[:, part], load_sem.at[i, 0]),
            pltpu.make_async_copy(lf_hbm.at[0, :, :, part], lf.at[i], load_sem.at[i, 1]),
            pltpu.make_async_copy(rp_hbm.at[0, :, part], rp.at[:, part], load_sem.at[i, 2]),
            pltpu.make_async_copy(rf_hbm.at[0, :, :, part], rf.at[i], load_sem.at[i, 3]),
        ]
        for copy in group:
            copy.start()
        loads.append(group)
    load_ids = pltpu.make_async_copy(ids_hbm, ids, ids_sem)
    load_ids.start()
    greet(rest)

    lane = lax.broadcasted_iota(jnp.int32, (8, LANES), 1) % GROUP
    own_id = jnp.where(lane < rows, (at["z"] * 8 + plane_slot) * rows + lane, -1)
    load_ids.wait()

    def count(i, counts):
        for j in range(8):
            counts = counts + jnp.where(own_id == ids[i * 8 + j], 1.0, 0.0)
        return counts

    counts = lax.fori_loop(0, val_count // 8, count, jnp.zeros((8, LANES), jnp.float32))[:1]

    left_part = jnp.zeros((32, used), jnp.float32)
    right_part = jnp.zeros((64, used), jnp.float32)
    for i in range(CHUNKS):
        for copy in loads[i]:
            copy.wait()
        part = slice(i * step, (i + 1) * step)
        left_part += dot(lp[:, part], lf[i].reshape(used, step), NT)
        right_part += dot(rp[:, part], rf[i].reshape(used, step), NT)
    own = jnp.concatenate([left_part, right_part], axis=0).astype(jnp.bfloat16)
    source = lax.broadcasted_iota(jnp.int32, (used, LANES), 0)
    goal = lax.broadcasted_iota(jnp.int32, (used, LANES), 1)
    place = jnp.where((source // rank == goal % GROUP) & (source % rank == goal // GROUP), 1.0, 0.0)
    own = dot(own, place.astype(jnp.bfloat16), NN).astype(jnp.bfloat16)
    blocks[slot] = own

    def send(stage, source, goal, peers):
        for peer in peers:
            pltpu.make_async_remote_copy(
                src_ref=source, dst_ref=goal, send_sem=send_sem.at[stage], recv_sem=recv_sem.at[stage],
                device_id=device(peer), device_id_type=MESH,
            ).start()

    def all_of(stage, view):
        return pltpu.make_async_remote_copy(
            src_ref=view, dst_ref=view, send_sem=send_sem.at[stage], recv_sem=recv_sem.at[stage],
            device_id=device(other), device_id_type=MESH,
        )

    def share(stage, buffer, index, value, peers):
        buffer[index] = value
        send(stage, buffer.at[index], buffer.at[index], peers)

    target = to_features(own[:32], own[32:], counts)
    pl.semaphore_wait(barrier, len(along_z) + len(plane) + 1)
    share(0, first, at["z"], target.astype(first.dtype), along_z)
    send(1, blocks.at[slot], blocks.at[slot], plane)
    all_of(0, first.at[pl.ds(0, 7)]).wait_recv()
    share(2, second, slot, jnp.sum(first[...].astype(jnp.float32), axis=0).astype(second.dtype), plane)
    all_of(1, blocks.at[pl.ds(0, 15)]).wait_recv()
    segment = lax.broadcasted_iota(jnp.int32, (96, LANES), 1) // GROUP
    for l in range(2):
        for h in range(2):
            four = [blocks[8 * l + 4 * h + j].astype(jnp.float32) for j in range(4)]
            for r in range(4):
                moves = [pltpu.roll(four[j], GROUP * ((j - r) % 4), 1) if j != r else four[j] for j in range(4)]
                value = jnp.where(
                    segment < 2, jnp.where(segment == 0, moves[0], moves[1]),
                    jnp.where(segment == 2, moves[2], moves[3]),
                )
                lanes = slice(256 * r + LANES * h, 256 * r + LANES * h + LANES)
                wide[l, :, lanes] = value.astype(jnp.bfloat16)
    left = [wide[l, :32] for l in range(2)]
    right = [wide[l, 32:] for l in range(2)]
    all_of(2, second.at[pl.ds(0, 15)]).wait_recv()
    target = [jnp.sum(second[pl.ds(8 * l, 8)].astype(jnp.float32), axis=0) for l in range(2)]

    def all_ranks(line):
        line = jnp.concatenate([line] * 4, axis=1)
        return [to_features(left[l], right[l], line) for l in range(2)]

    def send_features(index, values, scalars):
        share(6 + index, sums.at[index], at["z"], jnp.concatenate(values, axis=0).astype(jnp.bfloat16), along_z)
        share(8 + index, norms.at[index], at["z"], jnp.concatenate([halves(s) for s in scalars], axis=1), along_z)

    def take_features(index):
        all_of(6 + index, sums.at[index, pl.ds(0, 7)]).wait_recv()
        whole = jnp.sum(sums[index].astype(jnp.float32), axis=0)
        return [whole[:16], whole[16:]]

    def take_norms(index):
        all_of(8 + index, norms.at[index, pl.ds(0, 7)]).wait_recv()
        whole = jnp.sum(norms[index], axis=0)
        return total(whole[:, :LANES]), total(whole[:, LANES:])

    scale = 1.0 / (rank * total_features)
    align_scale = math.sqrt(val_count / total_features) / (val_count * rank)

    share(3, pair_0, at["c"], to_lanes(left, right, target, ranks_added), [other])
    all_of(3, pair_0.at[0]).wait_recv()
    start = (pair_0[0] + pair_0[1]) * align_scale
    start_parts = all_ranks(start)
    send_features(0, start_parts, [start * start, start])
    mixed = take_features(0)

    value = [to_lanes(left, right, mixed, ranks_added), products(mixed, mixed)]
    share(4, pair_1, at["c"], jnp.concatenate(value, axis=1), [other])
    norm, _ = take_norms(0)
    all_of(4, pair_1.at[0]).wait_recv()
    both = pair_1[0] + pair_1[1]
    product = both[:, :256]
    alpha = norm / (total(both[:, 256:]) * scale + RIDGE * norm)
    residual = start - alpha * (product * scale + RIDGE * start)
    parts = all_ranks(residual)
    send_features(1, parts, [residual * residual, residual * start])

    mine = lax.broadcasted_iota(jnp.int32, (1, 256), 1) // GROUP == plane_slot

    def own_row(value):
        return over_rank(halves(jnp.where(mine, value, 0.0)))

    mixed_square = total(both[:, 256:])
    start, residual, product = own_row(start), own_row(residual), own_row(product)
    weights = alpha * start
    left = [blocks[8 * l + plane_slot, :32] for l in range(2)]
    right = [blocks[8 * l + plane_slot, 32:] for l in range(2)]

    again = take_features(1)
    value = [to_lanes(left, right, again), products(again, again), products(again, mixed)]
    share(5, pair_2, at["c"], jnp.concatenate(value, axis=1), [other])
    norm_next, cross = take_norms(1)
    beta = norm_next / norm
    direction = residual + beta * start
    length = norm_next + 2.0 * beta * cross + beta * beta * norm
    all_of(5, pair_2.at[0]).wait_recv()
    both = pair_2[0] + pair_2[1]
    square = total(both[:, LANES:2 * LANES]) + 2.0 * beta * total(both[:, 2 * LANES:]) + beta * beta * mixed_square
    alpha = norm_next / (square * scale + RIDGE * length)
    image = (over_rank(both[:, :LANES]) + beta * product) * scale + RIDGE * direction
    out_ref[0:1] = weights + alpha * direction
    out_ref[1:2] = residual - alpha * image

    all_of(0, first.at[pl.ds(0, 7)]).wait_send()
    all_of(1, blocks.at[pl.ds(0, 15)]).wait_send()
    all_of(2, second.at[pl.ds(0, 15)]).wait_send()
    for i, pair in enumerate((pair_0, pair_1, pair_2)):
        all_of(3 + i, pair.at[0]).wait_send()
    for i in range(2):
        all_of(6 + i, sums.at[i, pl.ds(0, 7)]).wait_send()
        all_of(8 + i, norms.at[i, pl.ds(0, 7)]).wait_send()


def per_device(left_factors, right_factors, left_proj, right_proj, val_ids):
    _, rows, rank, width = left_factors.shape
    left_proj = jnp.swapaxes(left_proj, 1, 2)
    right_proj = jnp.swapaxes(right_proj, 1, 2)
    ka, kb = left_proj.shape[1], right_proj.shape[1]
    val_count = val_ids.shape[0]
    total_features = ka * kb * lax.axis_size("feat")
    step = width // CHUNKS
    operands = (left_factors, right_factors, left_proj, right_proj, val_ids)
    out = pl.pallas_call(
        functools.partial(kernel, rows, rank, total_features, val_count),
        out_shape=jax.ShapeDtypeStruct((2, LANES), jnp.float32),
        in_specs=[pl.BlockSpec(memory_space=pltpu.HBM)] * 5,
        out_specs=pl.BlockSpec(memory_space=pltpu.VMEM),
        scratch_shapes=[
            pltpu.VMEM((CHUNKS, rows, rank, step), jnp.bfloat16),
            pltpu.VMEM((CHUNKS, rows, rank, step), jnp.bfloat16),
            pltpu.VMEM((ka, width), jnp.bfloat16),
            pltpu.VMEM((kb, width), jnp.bfloat16),
            pltpu.SMEM((val_count,), jnp.int32),
            pltpu.VMEM((16, ka + kb, LANES), jnp.bfloat16),
            pltpu.VMEM((2, ka + kb, 8 * LANES), jnp.bfloat16),
            pltpu.VMEM((8, 16, LANES), jnp.bfloat16),
            pltpu.VMEM((16, 16, LANES), jnp.bfloat16),
            pltpu.VMEM((2, 8, 32, LANES), jnp.bfloat16),
            pltpu.VMEM((2, 8, 1, 2 * LANES), jnp.float32),
            pltpu.VMEM((2, 1, 2 * LANES), jnp.float32),
            pltpu.VMEM((2, 1, 3 * LANES), jnp.float32),
            pltpu.VMEM((2, 1, 3 * LANES), jnp.float32),
            pltpu.SemaphoreType.DMA((CHUNKS, 4)),
            pltpu.SemaphoreType.DMA,
            pltpu.SemaphoreType.DMA((10,)),
            pltpu.SemaphoreType.DMA((10,)),
        ],
        compiler_params=pltpu.CompilerParams(
            collective_id=0, has_side_effects=True, vmem_limit_bytes=32 * 2**20
        ),
        name="reweight",
    )(*(pltpu.with_memory_space_constraint(a, pltpu.HBM) for a in operands))
    return out[0, :rows], out[1, :rows]


def solution(mesh):
    return jax.shard_map(
        per_device,
        mesh=mesh,
        in_specs=(
            P("feat", "ex", None, None),
            P("feat", "ex", None, None),
            P("feat", None, None),
            P("feat", None, None),
            P(),
        ),
        out_specs=(P("ex"), P("ex")),
        check_vma=False,
    )
```

```python
import functools
import math

import jax
import jax.numpy as jnp
from jax import lax
from jax.experimental import pallas as pl
from jax.experimental.pallas import tpu as pltpu
from jax.sharding import PartitionSpec as P

MESH = pl.DeviceIdType.MESH
NT = (((1,), (1,)), ((), ()))
NN = (((1,), (0,)), ((), ()))
SIZE = dict(z=8, y=4, xh=2, xl=2, c=2)
RIDGE = 0.5
CHUNKS = 2
LANES = 128
GROUP = 32


def coordinates():
    ex = lax.axis_index("ex")
    feat = lax.axis_index("feat")
    return dict(z=ex // 8, y=(ex // 2) % 4, xh=ex % 2, xl=feat // 2, c=feat % 2)


def device(at):
    return (at["z"] * 8 + at["y"] * 2 + at["xh"], at["xl"] * 2 + at["c"])


def moved(at, **steps):
    new = dict(at)
    for axis, step in steps.items():
        if not isinstance(step, int) or step:
            new[axis] = (at[axis] + step) % SIZE[axis]
    return new


def hops(y, xh, xl):
    x = 2 * xh + xl
    return min(y, 4 - y) + min(x, 4 - x)


def split(value):
    high = value.astype(jnp.bfloat16)
    low = (value - high.astype(jnp.float32)).astype(jnp.bfloat16)
    return jnp.concatenate([high, low], axis=0)


def pack(value):
    return jnp.concatenate([value[:16], value[16:]], axis=1)


def unpack(value):
    return jnp.concatenate([value[:, :64], value[:, 64:]], axis=0)


def dot(a, b, dims):
    return lax.dot_general(a, b, dims, preferred_element_type=jnp.float32)


def to_features(left, right, row):
    sums = dot(split(left.astype(jnp.float32) * row), right, NT)
    return pack(sums[:32] + sums[32:])


def to_lanes(left, right, values, ranks=lambda term: term):
    total = None
    for l in range(2):
        mixed = dot(split(unpack(values[l])), right[l], NN)
        term = ranks((mixed[:32] + mixed[32:]) * left[l].astype(jnp.float32))
        total = term if total is None else total + term
    return jnp.sum(total, axis=0, keepdims=True)


def over_rank(rows):
    rows = rows + pltpu.roll(rows, 2 * GROUP, 1)
    return rows + pltpu.roll(rows, GROUP, 1)


def total(row):
    return jnp.sum(row, axis=1, keepdims=True)


def products(a, b):
    return jnp.sum(a[0] * b[0] + a[1] * b[1], axis=0, keepdims=True)


def halves(line):
    return line[:, :LANES] + line[:, LANES:]


def ranks_added(line):
    n = line.shape[1] // 4
    return (line[:, :n] + line[:, n:2 * n]) + (line[:, 2 * n:3 * n] + line[:, 3 * n:])


def kernel(
    rows, rank, total_features, val_count,
    lf_hbm, rf_hbm, lp_hbm, rp_hbm, ids_hbm, out_ref,
    lf, rf, lp, rp, ids, blocks, wide, first, second, sums, norms, pair_0, pair_1, pair_2,
    load_sem, ids_sem, send_sem, recv_sem,
):
    at = coordinates()
    width = lf_hbm.shape[3]
    step = width // CHUNKS
    used = rows * rank
    plane_slot = at["y"] * 2 + at["xh"]
    near = at["z"] % 2
    own_slot = (at["z"] // 2) * 2 + at["xh"]
    slot = at["xl"] * 8 + own_slot
    group_slot = at["y"] * 2 + near

    along_z = [moved(at, z=d) for d in (4, 3, 5, 2, 6, 1, 7)]
    plane = [(y, xh, xl) for y in range(4) for xh in range(2) for xl in range(2) if y or xh or xl]
    plane = [moved(at, y=y, xh=xh, xl=xl) for y, xh, xl in sorted(plane, key=lambda o: -hops(*o))]
    other = moved(at, c=1)
    along_x = [moved(at, xh=xh, xl=xl) for xh, xl in ((1, 0), (0, 1), (1, 1))]
    twins = [moved(at, y=y, z=1 - 2 * near) for y in (2, 1, 3, 0)]
    sharers = [twins[0], moved(at, y=2)] + twins[1:3] + [moved(at, y=1), moved(at, y=3), twins[3]]
    barrier = pltpu.get_barrier_semaphore()
    order = along_z[:1] + plane[:1] + along_z[1:3] + plane[1:5] + twins[:1]
    rest = along_z[3:] + plane[5:] + twins[1:3] + [other]

    def greet(peers):
        for peer in peers:
            pl.semaphore_signal(barrier, inc=1, device_id=device(peer), device_id_type=MESH)

    greet(order)

    loads = []
    for i in range(CHUNKS):
        part = pl.ds(i * step, step)
        group = [
            pltpu.make_async_copy(lp_hbm.at[0, :, part], lp.at[:, part], load_sem.at[i, 0]),
            pltpu.make_async_copy(lf_hbm.at[0, :, :, part], lf.at[i], load_sem.at[i, 1]),
            pltpu.make_async_copy(rp_hbm.at[0, :, part], rp.at[:, part], load_sem.at[i, 2]),
            pltpu.make_async_copy(rf_hbm.at[0, :, :, part], rf.at[i], load_sem.at[i, 3]),
        ]
        for copy in group:
            copy.start()
        loads.append(group)
    load_ids = pltpu.make_async_copy(ids_hbm, ids, ids_sem)
    load_ids.start()
    greet(rest)

    lane = lax.broadcasted_iota(jnp.int32, (8, LANES), 1) % GROUP
    own_id = jnp.where(lane < rows, (at["z"] * 8 + plane_slot) * rows + lane, -1)
    load_ids.wait()

    def count(i, counts):
        for j in range(8):
            counts = counts + jnp.where(own_id == ids[i * 8 + j], 1.0, 0.0)
        return counts

    counts = lax.fori_loop(0, val_count // 8, count, jnp.zeros((8, LANES), jnp.float32))[:1]

    left_part = jnp.zeros((32, used), jnp.float32)
    right_part = jnp.zeros((64, used), jnp.float32)
    for i in range(CHUNKS):
        for copy in loads[i]:
            copy.wait()
        part = slice(i * step, (i + 1) * step)
        left_part += dot(lp[:, part], lf[i].reshape(used, step), NT)
        right_part += dot(rp[:, part], rf[i].reshape(used, step), NT)
    own = jnp.concatenate([left_part, right_part], axis=0).astype(jnp.bfloat16)
    source = lax.broadcasted_iota(jnp.int32, (used, LANES), 0)
    goal = lax.broadcasted_iota(jnp.int32, (used, LANES), 1)
    place = jnp.where((source // rank == goal % GROUP) & (source % rank == goal // GROUP), 1.0, 0.0)
    own = dot(own, place.astype(jnp.bfloat16), NN).astype(jnp.bfloat16)
    blocks[slot] = own

    def send(stage, source, goal, peers):
        for peer in peers:
            pltpu.make_async_remote_copy(
                src_ref=source, dst_ref=goal, send_sem=send_sem.at[stage], recv_sem=recv_sem.at[stage],
                device_id=device(peer), device_id_type=MESH,
            ).start()

    def all_of(stage, view):
        return pltpu.make_async_remote_copy(
            src_ref=view, dst_ref=view, send_sem=send_sem.at[stage], recv_sem=recv_sem.at[stage],
            device_id=device(other), device_id_type=MESH,
        )

    def share(stage, buffer, index, value, peers):
        buffer[index] = value
        send(stage, buffer.at[index], buffer.at[index], peers)

    target = to_features(own[:32], own[32:], counts)
    pl.semaphore_wait(barrier, len(order) + len(rest))
    index = at["xl"] * 8 + plane_slot
    first[index] = target.astype(first.dtype)
    send(0, first.at[index], first.at[index], plane[:5])
    for d in (2, 1, 3):
        send(9 + d, blocks.at[slot], blocks.at[slot], [moved(at, z=2 * d)])
    send(0, first.at[index], first.at[index], plane[5:])
    send(1, blocks.at[slot], blocks.at[slot], along_x)

    def forward(d):
        come = at["xl"] * 8 + ((at["z"] // 2 + 4 - d) % 4) * 2 + at["xh"]
        all_of(9 + d, blocks.at[come]).wait_recv()
        send(1, blocks.at[come], blocks.at[come], along_x)

    forward(1)
    forward(3)
    all_of(0, first.at[pl.ds(0, 15)]).wait_recv()
    target = [jnp.sum(first[pl.ds(8 * l, 8)].astype(jnp.float32), axis=0) for l in range(2)]
    share(2, second, at["z"], jnp.concatenate(target, axis=0).astype(second.dtype), along_z)
    forward(2)
    all_of(1, blocks.at[pl.ds(0, 12)]).wait_recv()
    segment = lax.broadcasted_iota(jnp.int32, (96, LANES), 1) // GROUP
    for l in range(2):
        for h in range(2):
            four = [blocks[8 * l + 4 * h + j].astype(jnp.float32) for j in range(4)]
            for r in range(4):
                moves = [pltpu.roll(four[j], GROUP * ((j - r) % 4), 1) if j != r else four[j] for j in range(4)]
                value = jnp.where(
                    segment < 2, jnp.where(segment == 0, moves[0], moves[1]),
                    jnp.where(segment == 2, moves[2], moves[3]),
                )
                lanes = slice(256 * r + LANES * h, 256 * r + LANES * h + LANES)
                wide[l, :, lanes] = value.astype(jnp.bfloat16)
    left = [wide[l, :32] for l in range(2)]
    right = [wide[l, 32:] for l in range(2)]
    all_of(2, second.at[pl.ds(0, 7)]).wait_recv()
    target = jnp.sum(second[...].astype(jnp.float32), axis=0)
    target = [target[:16], target[16:]]

    def all_ranks(line):
        line = jnp.concatenate([line] * 4, axis=1)
        return [to_features(left[l], right[l], line) for l in range(2)]

    def send_features(index, values, scalars):
        share(6 + index, sums.at[index], group_slot, jnp.concatenate(values, axis=0).astype(jnp.bfloat16), sharers)
        share(8 + index, norms.at[index], group_slot, jnp.concatenate([halves(s) for s in scalars], axis=1), sharers)

    def take_features(index):
        all_of(6 + index, sums.at[index, pl.ds(0, 7)]).wait_recv()
        whole = jnp.sum(sums[index].astype(jnp.float32), axis=0)
        return [whole[:16], whole[16:]]

    def take_norms(index):
        all_of(8 + index, norms.at[index, pl.ds(0, 7)]).wait_recv()
        whole = jnp.sum(norms[index], axis=0)
        return total(whole[:, :LANES]), total(whole[:, LANES:])

    scale = 1.0 / (rank * total_features)
    align_scale = math.sqrt(val_count / total_features) / (val_count * rank)

    share(3, pair_0, at["c"], to_lanes(left, right, target, ranks_added), [other])
    all_of(3, pair_0.at[0]).wait_recv()
    start = (pair_0[0] + pair_0[1]) * align_scale
    start_parts = all_ranks(start)
    send_features(0, start_parts, [start * start, start])
    mixed = take_features(0)

    value = [to_lanes(left, right, mixed, ranks_added), products(mixed, mixed)]
    share(4, pair_1, at["c"], jnp.concatenate(value, axis=1), [other])
    norm, _ = take_norms(0)
    all_of(4, pair_1.at[0]).wait_recv()
    both = pair_1[0] + pair_1[1]
    product = both[:, :256]
    alpha = norm / (total(both[:, 256:]) * scale + RIDGE * norm)
    residual = start - alpha * (product * scale + RIDGE * start)
    parts = all_ranks(residual)
    send_features(1, parts, [residual * residual, residual * start])

    mine = lax.broadcasted_iota(jnp.int32, (1, 256), 1) // GROUP == own_slot

    def own_row(value):
        return over_rank(halves(jnp.where(mine, value, 0.0)))

    mixed_square = total(both[:, 256:])
    start, residual, product = own_row(start), own_row(residual), own_row(product)
    weights = alpha * start
    left = [blocks[8 * l + own_slot, :32] for l in range(2)]
    right = [blocks[8 * l + own_slot, 32:] for l in range(2)]

    again = take_features(1)
    value = [to_lanes(left, right, again), products(again, again), products(again, mixed)]
    share(5, pair_2, at["c"], jnp.concatenate(value, axis=1), [other])
    norm_next, cross = take_norms(1)
    beta = norm_next / norm
    direction = residual + beta * start
    length = norm_next + 2.0 * beta * cross + beta * beta * norm
    all_of(5, pair_2.at[0]).wait_recv()
    both = pair_2[0] + pair_2[1]
    square = total(both[:, LANES:2 * LANES]) + 2.0 * beta * total(both[:, 2 * LANES:]) + beta * beta * mixed_square
    alpha = norm_next / (square * scale + RIDGE * length)
    image = (over_rank(both[:, :LANES]) + beta * product) * scale + RIDGE * direction
    out_ref[0:1] = weights + alpha * direction
    out_ref[1:2] = residual - alpha * image

    all_of(0, first.at[pl.ds(0, 15)]).wait_send()
    all_of(1, blocks.at[pl.ds(0, 12)]).wait_send()
    for d in (1, 2, 3):
        all_of(9 + d, blocks.at[0]).wait_send()
    all_of(2, second.at[pl.ds(0, 7)]).wait_send()
    for i, pair in enumerate((pair_0, pair_1, pair_2)):
        all_of(3 + i, pair.at[0]).wait_send()
    for i in range(2):
        all_of(6 + i, sums.at[i, pl.ds(0, 7)]).wait_send()
        all_of(8 + i, norms.at[i, pl.ds(0, 7)]).wait_send()


def per_device(left_factors, right_factors, left_proj, right_proj, val_ids):
    _, rows, rank, width = left_factors.shape
    left_proj = jnp.swapaxes(left_proj, 1, 2)
    right_proj = jnp.swapaxes(right_proj, 1, 2)
    ka, kb = left_proj.shape[1], right_proj.shape[1]
    val_count = val_ids.shape[0]
    total_features = ka * kb * lax.axis_size("feat")
    step = width // CHUNKS
    operands = (left_factors, right_factors, left_proj, right_proj, val_ids)
    out = pl.pallas_call(
        functools.partial(kernel, rows, rank, total_features, val_count),
        out_shape=jax.ShapeDtypeStruct((2, LANES), jnp.float32),
        in_specs=[pl.BlockSpec(memory_space=pltpu.HBM)] * 5,
        out_specs=pl.BlockSpec(memory_space=pltpu.VMEM),
        scratch_shapes=[
            pltpu.VMEM((CHUNKS, rows, rank, step), jnp.bfloat16),
            pltpu.VMEM((CHUNKS, rows, rank, step), jnp.bfloat16),
            pltpu.VMEM((ka, width), jnp.bfloat16),
            pltpu.VMEM((kb, width), jnp.bfloat16),
            pltpu.SMEM((val_count,), jnp.int32),
            pltpu.VMEM((16, ka + kb, LANES), jnp.bfloat16),
            pltpu.VMEM((2, ka + kb, 8 * LANES), jnp.bfloat16),
            pltpu.VMEM((16, 16, LANES), jnp.bfloat16),
            pltpu.VMEM((8, 32, LANES), jnp.bfloat16),
            pltpu.VMEM((2, 8, 32, LANES), jnp.bfloat16),
            pltpu.VMEM((2, 8, 1, 2 * LANES), jnp.float32),
            pltpu.VMEM((2, 1, 2 * LANES), jnp.float32),
            pltpu.VMEM((2, 1, 3 * LANES), jnp.float32),
            pltpu.VMEM((2, 1, 3 * LANES), jnp.float32),
            pltpu.SemaphoreType.DMA((CHUNKS, 4)),
            pltpu.SemaphoreType.DMA,
            pltpu.SemaphoreType.DMA((13,)),
            pltpu.SemaphoreType.DMA((13,)),
        ],
        compiler_params=pltpu.CompilerParams(
            collective_id=0, has_side_effects=True, vmem_limit_bytes=32 * 2**20
        ),
        name="reweight",
    )(*(pltpu.with_memory_space_constraint(a, pltpu.HBM) for a in operands))
    return out[0, :rows], out[1, :rows]


def solution(mesh):
    return jax.shard_map(
        per_device,
        mesh=mesh,
        in_specs=(
            P("feat", "ex", None, None),
            P("feat", "ex", None, None),
            P("feat", None, None),
            P("feat", None, None),
            P(),
        ),
        out_specs=(P("ex"), P("ex")),
        check_vma=False,
    )
```

```python
import functools
import math

import jax
import jax.numpy as jnp
from jax import lax
from jax.experimental import pallas as pl
from jax.experimental.pallas import tpu as pltpu
from jax.sharding import PartitionSpec as P

MESH = pl.DeviceIdType.MESH
NT = (((1,), (1,)), ((), ()))
NN = (((1,), (0,)), ((), ()))
SIZE = dict(z=8, y=4, xh=2, xl=2, c=2)
RIDGE = 0.5
CHUNKS = 4
LANES = 128
GROUP = 32


def coordinates():
    ex = lax.axis_index("ex")
    feat = lax.axis_index("feat")
    return dict(z=ex // 8, y=(ex // 2) % 4, xh=ex % 2, xl=feat // 2, c=feat % 2)


def device(at):
    return (at["z"] * 8 + at["y"] * 2 + at["xh"], at["xl"] * 2 + at["c"])


def moved(at, **steps):
    new = dict(at)
    for axis, step in steps.items():
        if not isinstance(step, int) or step:
            new[axis] = (at[axis] + step) % SIZE[axis]
    return new


def hops(y, xh, xl):
    x = 2 * xh + xl
    return min(y, 4 - y) + min(x, 4 - x)


def split(value):
    high = value.astype(jnp.bfloat16)
    low = (value - high.astype(jnp.float32)).astype(jnp.bfloat16)
    return jnp.concatenate([high, low], axis=0)


def pack(value):
    return jnp.concatenate([value[:16], value[16:]], axis=1)


def unpack(value):
    return jnp.concatenate([value[:, :64], value[:, 64:]], axis=0)


def dot(a, b, dims):
    return lax.dot_general(a, b, dims, preferred_element_type=jnp.float32)


def to_features(left, right, row):
    sums = dot(split(left.astype(jnp.float32) * row), right, NT)
    return pack(sums[:32] + sums[32:])


def to_lanes(left, right, values, ranks=lambda term: term):
    total = None
    for l in range(2):
        mixed = dot(split(unpack(values[l])), right[l], NN)
        term = ranks((mixed[:32] + mixed[32:]) * left[l].astype(jnp.float32))
        total = term if total is None else total + term
    return jnp.sum(total, axis=0, keepdims=True)


def over_rank(rows):
    rows = rows + pltpu.roll(rows, 2 * GROUP, 1)
    return rows + pltpu.roll(rows, GROUP, 1)


def total(row):
    return jnp.sum(row, axis=1, keepdims=True)


def products(a, b):
    return jnp.sum(a[0] * b[0] + a[1] * b[1], axis=0, keepdims=True)


def halves(line):
    return line[:, :LANES] + line[:, LANES:]


def ranks_added(line):
    n = line.shape[1] // 4
    return (line[:, :n] + line[:, n:2 * n]) + (line[:, 2 * n:3 * n] + line[:, 3 * n:])


def kernel(
    rows, rank, total_features, val_count,
    lf_hbm, rf_hbm, lp_hbm, rp_hbm, ids_hbm, out_ref,
    lf, rf, lp, rp, ids, blocks, wide, first, second, sums, norms, pair_0, pair_1, pair_2,
    load_sem, ids_sem, send_sem, recv_sem,
):
    at = coordinates()
    width = lf_hbm.shape[3]
    step = width // CHUNKS
    used = rows * rank
    plane_slot = at["y"] * 2 + at["xh"]
    near = at["z"] % 2
    own_slot = at["xh"]
    slot = at["xl"] * 8 + own_slot
    group_slot = at["y"] * 2 + near

    along_z = [moved(at, z=d) for d in (4, 3, 5, 2, 6, 1, 7)]
    plane = [(y, xh, xl) for y in range(4) for xh in range(2) for xl in range(2) if y or xh or xl]
    plane = [moved(at, y=y, xh=xh, xl=xl) for y, xh, xl in sorted(plane, key=lambda o: -hops(*o))]
    other = moved(at, c=1)
    along_x = [moved(at, xh=xh, xl=xl) for xh, xl in ((1, 0), (0, 1), (1, 1))]
    twins = [moved(at, y=y, z=1 - 2 * near) for y in (2, 1, 3, 0)]
    sharers = [twins[0], moved(at, y=2)] + twins[1:3] + [moved(at, y=1), moved(at, y=3), twins[3]]
    barrier = pltpu.get_barrier_semaphore()
    order = along_z[:1] + plane[:1] + along_z[1:3] + plane[1:5] + twins[:1]
    rest = along_z[3:] + plane[5:] + twins[1:3] + [other]

    def greet(peers):
        for peer in peers:
            pl.semaphore_signal(barrier, inc=1, device_id=device(peer), device_id_type=MESH)

    greet(order)

    loads = []
    for i in range(CHUNKS):
        part = pl.ds(i * step, step)
        group = [
            pltpu.make_async_copy(lp_hbm.at[0, :, part], lp.at[:, part], load_sem.at[i, 0]),
            pltpu.make_async_copy(lf_hbm.at[0, :, :, part], lf.at[i], load_sem.at[i, 1]),
            pltpu.make_async_copy(rp_hbm.at[0, :, part], rp.at[:, part], load_sem.at[i, 2]),
            pltpu.make_async_copy(rf_hbm.at[0, :, :, part], rf.at[i], load_sem.at[i, 3]),
        ]
        for copy in group:
            copy.start()
        loads.append(group)
    load_ids = pltpu.make_async_copy(ids_hbm, ids, ids_sem)
    load_ids.start()
    greet(rest)

    lane = lax.broadcasted_iota(jnp.int32, (8, LANES), 1) % GROUP
    own_id = jnp.where(lane < rows, (at["z"] * 8 + plane_slot) * rows + lane, -1)
    load_ids.wait()

    def count(i, counts):
        for j in range(8):
            counts = counts + jnp.where(own_id == ids[i * 8 + j], 1.0, 0.0)
        return counts

    counts = lax.fori_loop(0, val_count // 8, count, jnp.zeros((8, LANES), jnp.float32))[:1]

    left_part = jnp.zeros((32, used), jnp.float32)
    right_part = jnp.zeros((64, used), jnp.float32)
    for i in range(CHUNKS):
        for copy in loads[i]:
            copy.wait()
        part = slice(i * step, (i + 1) * step)
        left_part += dot(lp[:, part], lf[i].reshape(used, step), NT)
        right_part += dot(rp[:, part], rf[i].reshape(used, step), NT)
    own = jnp.concatenate([left_part, right_part], axis=0).astype(jnp.bfloat16)
    source = lax.broadcasted_iota(jnp.int32, (used, LANES), 0)
    goal = lax.broadcasted_iota(jnp.int32, (used, LANES), 1)
    place = jnp.where((source // rank == goal % GROUP) & (source % rank == goal // GROUP), 1.0, 0.0)
    own = dot(own, place.astype(jnp.bfloat16), NN).astype(jnp.bfloat16)
    blocks[slot] = own

    def send(stage, source, goal, peers):
        for peer in peers:
            pltpu.make_async_remote_copy(
                src_ref=source, dst_ref=goal, send_sem=send_sem.at[stage], recv_sem=recv_sem.at[stage],
                device_id=device(peer), device_id_type=MESH,
            ).start()

    def all_of(stage, view):
        return pltpu.make_async_remote_copy(
            src_ref=view, dst_ref=view, send_sem=send_sem.at[stage], recv_sem=recv_sem.at[stage],
            device_id=device(other), device_id_type=MESH,
        )

    def share(stage, buffer, index, value, peers):
        buffer[index] = value
        send(stage, buffer.at[index], buffer.at[index], peers)

    target = to_features(own[:32], own[32:], counts)
    pl.semaphore_wait(barrier, len(order) + len(rest))
    place_of = {1: 1, 3: 2, 2: 3}
    index = at["xl"] * 8 + plane_slot
    first[index] = target.astype(first.dtype)
    send(0, first.at[index], first.at[index], plane[:5])
    for d in (2, 1, 3):
        send(9 + d, blocks.at[slot], blocks.at[slot + 2 * place_of[d]], [moved(at, z=2 * d)])
    send(0, first.at[index], first.at[index], plane[5:])
    send(1, blocks.at[slot], blocks.at[slot], along_x)

    def forward(d):
        come = slot + 2 * place_of[d]
        all_of(9 + d, blocks.at[come]).wait_recv()
        send(1 if d == 1 else 13, blocks.at[come], blocks.at[come], along_x)

    def lay_out(h):
        for l in range(2):
            four = [blocks[8 * l + 4 * h + j].astype(jnp.float32) for j in range(4)]
            for r in range(4):
                moves = [pltpu.roll(four[j], GROUP * ((j - r) % 4), 1) if j != r else four[j] for j in range(4)]
                value = jnp.where(
                    segment < 2, jnp.where(segment == 0, moves[0], moves[1]),
                    jnp.where(segment == 2, moves[2], moves[3]),
                )
                lanes = slice(256 * r + LANES * h, 256 * r + LANES * h + LANES)
                wide[l, :, lanes] = value.astype(jnp.bfloat16)

    segment = lax.broadcasted_iota(jnp.int32, (96, LANES), 1) // GROUP
    forward(1)
    forward(3)
    all_of(0, first.at[pl.ds(0, 15)]).wait_recv()
    target = [jnp.sum(first[pl.ds(8 * l, 8)].astype(jnp.float32), axis=0) for l in range(2)]
    share(2, second, at["z"], jnp.concatenate(target, axis=0).astype(second.dtype), along_z)
    forward(2)
    all_of(1, blocks.at[pl.ds(0, 6)]).wait_recv()
    lay_out(0)
    all_of(13, blocks.at[pl.ds(0, 6)]).wait_recv()
    lay_out(1)
    left = [wide[l, :32] for l in range(2)]
    right = [wide[l, 32:] for l in range(2)]
    all_of(2, second.at[pl.ds(0, 7)]).wait_recv()
    target = jnp.sum(second[...].astype(jnp.float32), axis=0)
    target = [target[:16], target[16:]]

    def all_ranks(line):
        line = jnp.concatenate([line] * 4, axis=1)
        return [to_features(left[l], right[l], line) for l in range(2)]

    def send_features(index, values, scalars):
        share(6 + index, sums.at[index], group_slot, jnp.concatenate(values, axis=0).astype(jnp.bfloat16), sharers)
        share(8 + index, norms.at[index], group_slot, jnp.concatenate([halves(s) for s in scalars], axis=1), sharers)

    def take_features(index):
        all_of(6 + index, sums.at[index, pl.ds(0, 7)]).wait_recv()
        whole = jnp.sum(sums[index].astype(jnp.float32), axis=0)
        return [whole[:16], whole[16:]]

    def take_norms(index):
        all_of(8 + index, norms.at[index, pl.ds(0, 7)]).wait_recv()
        whole = jnp.sum(norms[index], axis=0)
        return total(whole[:, :LANES]), total(whole[:, LANES:])

    scale = 1.0 / (rank * total_features)
    align_scale = math.sqrt(val_count / total_features) / (val_count * rank)

    share(3, pair_0, at["c"], to_lanes(left, right, target, ranks_added), [other])
    all_of(3, pair_0.at[0]).wait_recv()
    start = (pair_0[0] + pair_0[1]) * align_scale
    start_parts = all_ranks(start)
    send_features(0, start_parts, [start * start, start])
    mixed = take_features(0)

    value = [to_lanes(left, right, mixed, ranks_added), products(mixed, mixed)]
    share(4, pair_1, at["c"], jnp.concatenate(value, axis=1), [other])
    norm, _ = take_norms(0)
    all_of(4, pair_1.at[0]).wait_recv()
    both = pair_1[0] + pair_1[1]
    product = both[:, :256]
    alpha = norm / (total(both[:, 256:]) * scale + RIDGE * norm)
    residual = start - alpha * (product * scale + RIDGE * start)
    parts = all_ranks(residual)
    send_features(1, parts, [residual * residual, residual * start])

    mine = lax.broadcasted_iota(jnp.int32, (1, 256), 1) // GROUP == own_slot

    def own_row(value):
        return over_rank(halves(jnp.where(mine, value, 0.0)))

    mixed_square = total(both[:, 256:])
    start, residual, product = own_row(start), own_row(residual), own_row(product)
    weights = alpha * start
    left = [blocks[8 * l + own_slot, :32] for l in range(2)]
    right = [blocks[8 * l + own_slot, 32:] for l in range(2)]

    again = take_features(1)
    value = [to_lanes(left, right, again), products(again, again), products(again, mixed)]
    share(5, pair_2, at["c"], jnp.concatenate(value, axis=1), [other])
    norm_next, cross = take_norms(1)
    beta = norm_next / norm
    direction = residual + beta * start
    length = norm_next + 2.0 * beta * cross + beta * beta * norm
    all_of(5, pair_2.at[0]).wait_recv()
    both = pair_2[0] + pair_2[1]
    square = total(both[:, LANES:2 * LANES]) + 2.0 * beta * total(both[:, 2 * LANES:]) + beta * beta * mixed_square
    alpha = norm_next / (square * scale + RIDGE * length)
    image = (over_rank(both[:, :LANES]) + beta * product) * scale + RIDGE * direction
    out_ref[0:1] = weights + alpha * direction
    out_ref[1:2] = residual - alpha * image

    all_of(0, first.at[pl.ds(0, 15)]).wait_send()
    all_of(1, blocks.at[pl.ds(0, 6)]).wait_send()
    all_of(13, blocks.at[pl.ds(0, 6)]).wait_send()
    for d in (1, 2, 3):
        all_of(9 + d, blocks.at[0]).wait_send()
    all_of(2, second.at[pl.ds(0, 7)]).wait_send()
    for i, pair in enumerate((pair_0, pair_1, pair_2)):
        all_of(3 + i, pair.at[0]).wait_send()
    for i in range(2):
        all_of(6 + i, sums.at[i, pl.ds(0, 7)]).wait_send()
        all_of(8 + i, norms.at[i, pl.ds(0, 7)]).wait_send()


def per_device(left_factors, right_factors, left_proj, right_proj, val_ids):
    _, rows, rank, width = left_factors.shape
    left_proj = jnp.swapaxes(left_proj, 1, 2)
    right_proj = jnp.swapaxes(right_proj, 1, 2)
    ka, kb = left_proj.shape[1], right_proj.shape[1]
    val_count = val_ids.shape[0]
    total_features = ka * kb * lax.axis_size("feat")
    step = width // CHUNKS
    operands = (left_factors, right_factors, left_proj, right_proj, val_ids)
    out = pl.pallas_call(
        functools.partial(kernel, rows, rank, total_features, val_count),
        out_shape=jax.ShapeDtypeStruct((2, LANES), jnp.float32),
        in_specs=[pl.BlockSpec(memory_space=pltpu.HBM)] * 5,
        out_specs=pl.BlockSpec(memory_space=pltpu.VMEM),
        scratch_shapes=[
            pltpu.VMEM((CHUNKS, rows, rank, step), jnp.bfloat16),
            pltpu.VMEM((CHUNKS, rows, rank, step), jnp.bfloat16),
            pltpu.VMEM((ka, width), jnp.bfloat16),
            pltpu.VMEM((kb, width), jnp.bfloat16),
            pltpu.SMEM((val_count,), jnp.int32),
            pltpu.VMEM((16, ka + kb, LANES), jnp.bfloat16),
            pltpu.VMEM((2, ka + kb, 8 * LANES), jnp.bfloat16),
            pltpu.VMEM((16, 16, LANES), jnp.bfloat16),
            pltpu.VMEM((8, 32, LANES), jnp.bfloat16),
            pltpu.VMEM((2, 8, 32, LANES), jnp.bfloat16),
            pltpu.VMEM((2, 8, 1, 2 * LANES), jnp.float32),
            pltpu.VMEM((2, 1, 2 * LANES), jnp.float32),
            pltpu.VMEM((2, 1, 3 * LANES), jnp.float32),
            pltpu.VMEM((2, 1, 3 * LANES), jnp.float32),
            pltpu.SemaphoreType.DMA((CHUNKS, 4)),
            pltpu.SemaphoreType.DMA,
            pltpu.SemaphoreType.DMA((14,)),
            pltpu.SemaphoreType.DMA((14,)),
        ],
        compiler_params=pltpu.CompilerParams(
            collective_id=0, has_side_effects=True, vmem_limit_bytes=32 * 2**20
        ),
        name="reweight",
    )(*(pltpu.with_memory_space_constraint(a, pltpu.HBM) for a in operands))
    return out[0, :rows], out[1, :rows]


def solution(mesh):
    return jax.shard_map(
        per_device,
        mesh=mesh,
        in_specs=(
            P("feat", "ex", None, None),
            P("feat", "ex", None, None),
            P("feat", None, None),
            P("feat", None, None),
            P(),
        ),
        out_specs=(P("ex"), P("ex")),
        check_vma=False,
    )
```

```python
import functools
import math

import jax
import jax.numpy as jnp
from jax import lax
from jax.experimental import pallas as pl
from jax.experimental.pallas import tpu as pltpu
from jax.sharding import PartitionSpec as P

MESH = pl.DeviceIdType.MESH
NT = (((1,), (1,)), ((), ()))
NN = (((1,), (0,)), ((), ()))
SIZE = dict(z=8, y=4, xh=2, xl=2, c=2)
RIDGE = 0.5
CHUNKS = 4
LANES = 128
GROUP = 32


def coordinates():
    ex = lax.axis_index("ex")
    feat = lax.axis_index("feat")
    return dict(z=ex // 8, y=(ex // 2) % 4, xh=ex % 2, xl=feat // 2, c=feat % 2)


def device(at):
    return (at["z"] * 8 + at["y"] * 2 + at["xh"], at["xl"] * 2 + at["c"])


def moved(at, **steps):
    new = dict(at)
    for axis, step in steps.items():
        if not isinstance(step, int) or step:
            new[axis] = (at[axis] + step) % SIZE[axis]
    return new


def hops(y, xh, xl):
    x = 2 * xh + xl
    return min(y, 4 - y) + min(x, 4 - x)


def split(value):
    high = value.astype(jnp.bfloat16)
    low = (value - high.astype(jnp.float32)).astype(jnp.bfloat16)
    return jnp.concatenate([high, low], axis=0)


def pack(value):
    return jnp.concatenate([value[:16], value[16:]], axis=1)


def low_lanes(rows):
    return lax.broadcasted_iota(jnp.int32, (rows, LANES), 1) < LANES // 2


def side_by_side(first, second):
    low = low_lanes(16)
    top = jnp.where(low, first, pltpu.roll(second, LANES // 2, 1))
    bottom = jnp.where(low, pltpu.roll(first, LANES // 2, 1), second)
    return jnp.concatenate([top, bottom], axis=0)


def dot(a, b, dims):
    return lax.dot_general(a, b, dims, preferred_element_type=jnp.float32)


def to_features(left, right, row):
    sums = dot(split(left.astype(jnp.float32) * row), right, NT)
    return pack(sums[:32] + sums[32:])


def to_lanes(left, right, values, ranks=lambda term: term):
    low = low_lanes(32)
    both = jnp.concatenate([split(jnp.where(low, values, 0.0)), split(jnp.where(low, 0.0, values))], axis=0)
    mixed = dot(both, right, NN)
    total = ranks((mixed[:32] + mixed[32:64]) * left[0].astype(jnp.float32))
    total += ranks((mixed[64:96] + mixed[96:]) * left[1].astype(jnp.float32))
    return jnp.sum(total, axis=0, keepdims=True)


def over_rank(rows):
    rows = rows + pltpu.roll(rows, 2 * GROUP, 1)
    return rows + pltpu.roll(rows, GROUP, 1)


def total(row):
    return jnp.sum(row, axis=1, keepdims=True)


def products(a, b):
    return jnp.sum(a * b, axis=0, keepdims=True)


def halves(line):
    return line[:, :LANES] + line[:, LANES:]


def ranks_added(line):
    n = line.shape[1] // 4
    return (line[:, :n] + line[:, n:2 * n]) + (line[:, 2 * n:3 * n] + line[:, 3 * n:])


def kernel(
    rows, rank, total_features, val_count,
    lf_hbm, rf_hbm, lp_hbm, rp_hbm, ids_hbm, out_ref,
    lf, rf, lp, rp, ids, blocks, wide_left, wide_right, first, second, sums, norms, pair_0, pair_1, pair_2,
    load_sem, ids_sem, send_sem, recv_sem,
):
    at = coordinates()
    width = lf_hbm.shape[3]
    step = width // CHUNKS
    used = rows * rank
    plane_slot = at["y"] * 2 + at["xh"]
    near = at["z"] % 2
    own_slot = at["xh"]
    slot = at["xl"] * 8 + own_slot
    group_slot = at["y"] * 2 + near

    along_z = [moved(at, z=d) for d in (4, 3, 5, 2, 6, 1, 7)]
    plane = [(y, xh, xl) for y in range(4) for xh in range(2) for xl in range(2) if y or xh or xl]
    plane = [moved(at, y=y, xh=xh, xl=xl) for y, xh, xl in sorted(plane, key=lambda o: -hops(*o))]
    other = moved(at, c=1)
    along_x = [moved(at, xh=xh, xl=xl) for xh, xl in ((1, 0), (0, 1), (1, 1))]
    twins = [moved(at, y=y, z=1 - 2 * near) for y in (2, 1, 3, 0)]
    sharers = [twins[0], moved(at, y=2)] + twins[1:3] + [moved(at, y=1), moved(at, y=3), twins[3]]
    barrier = pltpu.get_barrier_semaphore()
    order = along_z[:1] + plane[:1] + along_z[1:3] + plane[1:5] + twins[:1]
    rest = along_z[3:] + plane[5:] + twins[1:3] + [other]

    def greet(peers):
        for peer in peers:
            pl.semaphore_signal(barrier, inc=1, device_id=device(peer), device_id_type=MESH)

    greet(order)

    loads = []
    for i in range(CHUNKS):
        part = pl.ds(i * step, step)
        group = [
            pltpu.make_async_copy(lp_hbm.at[0, :, part], lp.at[:, part], load_sem.at[i, 0]),
            pltpu.make_async_copy(lf_hbm.at[0, :, :, part], lf.at[i], load_sem.at[i, 1]),
            pltpu.make_async_copy(rp_hbm.at[0, :, part], rp.at[:, part], load_sem.at[i, 2]),
            pltpu.make_async_copy(rf_hbm.at[0, :, :, part], rf.at[i], load_sem.at[i, 3]),
        ]
        for copy in group:
            copy.start()
        loads.append(group)
    load_ids = pltpu.make_async_copy(ids_hbm, ids, ids_sem)
    load_ids.start()
    greet(rest)

    lane = lax.broadcasted_iota(jnp.int32, (8, LANES), 1) % GROUP
    own_id = jnp.where(lane < rows, (at["z"] * 8 + plane_slot) * rows + lane, -1)
    load_ids.wait()

    def count(i, counts):
        for j in range(8):
            counts = counts + jnp.where(own_id == ids[i * 8 + j], 1.0, 0.0)
        return counts

    counts = lax.fori_loop(0, val_count // 8, count, jnp.zeros((8, LANES), jnp.float32))[:1]

    left_part = jnp.zeros((32, used), jnp.float32)
    right_part = jnp.zeros((64, used), jnp.float32)
    for i in range(CHUNKS):
        for copy in loads[i]:
            copy.wait()
        part = slice(i * step, (i + 1) * step)
        left_part += dot(lp[:, part], lf[i].reshape(used, step), NT)
        right_part += dot(rp[:, part], rf[i].reshape(used, step), NT)
    own = jnp.concatenate([left_part, right_part], axis=0).astype(jnp.bfloat16)
    source = lax.broadcasted_iota(jnp.int32, (used, LANES), 0)
    goal = lax.broadcasted_iota(jnp.int32, (used, LANES), 1)
    place = jnp.where((source // rank == goal % GROUP) & (source % rank == goal // GROUP), 1.0, 0.0)
    own = dot(own, place.astype(jnp.bfloat16), NN).astype(jnp.bfloat16)
    blocks[slot] = own

    def send(stage, source, goal, peers):
        for peer in peers:
            pltpu.make_async_remote_copy(
                src_ref=source, dst_ref=goal, send_sem=send_sem.at[stage], recv_sem=recv_sem.at[stage],
                device_id=device(peer), device_id_type=MESH,
            ).start()

    def all_of(stage, view):
        return pltpu.make_async_remote_copy(
            src_ref=view, dst_ref=view, send_sem=send_sem.at[stage], recv_sem=recv_sem.at[stage],
            device_id=device(other), device_id_type=MESH,
        )

    def share(stage, buffer, index, value, peers):
        buffer[index] = value
        send(stage, buffer.at[index], buffer.at[index], peers)

    target = to_features(own[:32], own[32:], counts)
    pl.semaphore_wait(barrier, len(order) + len(rest))
    place_of = {1: 1, 3: 2, 2: 3}
    index = at["xl"] * 8 + plane_slot
    first[index] = target.astype(first.dtype)
    send(0, first.at[index], first.at[index], plane[:5])
    for d in (2, 1, 3):
        send(9 + d, blocks.at[slot], blocks.at[slot + 2 * place_of[d]], [moved(at, z=2 * d)])
    send(0, first.at[index], first.at[index], plane[5:])
    send(1, blocks.at[slot], blocks.at[slot], along_x)

    def forward(d):
        come = slot + 2 * place_of[d]
        all_of(9 + d, blocks.at[come]).wait_recv()
        send(1 if d == 1 else 13, blocks.at[come], blocks.at[come], along_x)

    def lay_out(h):
        for l in range(2):
            four = [blocks[8 * l + 4 * h + j].astype(jnp.float32) for j in range(4)]
            for r in range(4):
                moves = [pltpu.roll(four[j], GROUP * ((j - r) % 4), 1) if j != r else four[j] for j in range(4)]
                value = jnp.where(
                    segment < 2, jnp.where(segment == 0, moves[0], moves[1]),
                    jnp.where(segment == 2, moves[2], moves[3]),
                )
                lanes = slice(256 * r + LANES * h, 256 * r + LANES * h + LANES)
                wide_left[pl.ds(32 * l, 32), lanes] = value[:32].astype(jnp.bfloat16)
                wide_right[pl.ds(64 * l, 64), lanes] = value[32:].astype(jnp.bfloat16)

    segment = lax.broadcasted_iota(jnp.int32, (96, LANES), 1) // GROUP
    forward(1)
    forward(3)
    all_of(0, first.at[pl.ds(0, 15)]).wait_recv()
    target = [jnp.sum(first[pl.ds(8 * l, 8)].astype(jnp.float32), axis=0) for l in range(2)]
    share(2, second, at["z"], side_by_side(*target).astype(second.dtype), along_z)
    forward(2)
    all_of(1, blocks.at[pl.ds(0, 6)]).wait_recv()
    lay_out(0)
    all_of(13, blocks.at[pl.ds(0, 6)]).wait_recv()
    lay_out(1)
    left = [wide_left[:32], wide_left[32:]]
    right = wide_right[...]
    all_of(2, second.at[pl.ds(0, 7)]).wait_recv()
    target = jnp.sum(second[...].astype(jnp.float32), axis=0)

    def all_ranks(line):
        line = jnp.concatenate([line] * 4, axis=1)
        both = jnp.concatenate([split(left[l].astype(jnp.float32) * line) for l in range(2)], axis=0)
        parts = dot(both, right, NT)
        return jnp.where(low_lanes(32), parts[:32] + parts[32:64], parts[64:96] + parts[96:])

    def send_features(index, values, scalars):
        share(6 + index, sums.at[index], group_slot, values.astype(jnp.bfloat16), sharers)
        share(8 + index, norms.at[index], group_slot, jnp.concatenate([halves(s) for s in scalars], axis=1), sharers)

    def take_features(index):
        all_of(6 + index, sums.at[index, pl.ds(0, 7)]).wait_recv()
        return jnp.sum(sums[index].astype(jnp.float32), axis=0)

    def take_norms(index):
        all_of(8 + index, norms.at[index, pl.ds(0, 7)]).wait_recv()
        whole = jnp.sum(norms[index], axis=0)
        return total(whole[:, :LANES]), total(whole[:, LANES:])

    scale = 1.0 / (rank * total_features)
    align_scale = math.sqrt(val_count / total_features) / (val_count * rank)

    share(3, pair_0, at["c"], to_lanes(left, right, target, ranks_added), [other])
    all_of(3, pair_0.at[0]).wait_recv()
    start = (pair_0[0] + pair_0[1]) * align_scale
    start_parts = all_ranks(start)
    send_features(0, start_parts, [start * start, start])
    mixed = take_features(0)

    value = [to_lanes(left, right, mixed, ranks_added), products(mixed, mixed)]
    share(4, pair_1, at["c"], jnp.concatenate(value, axis=1), [other])
    norm, _ = take_norms(0)
    all_of(4, pair_1.at[0]).wait_recv()
    both = pair_1[0] + pair_1[1]
    product = both[:, :256]
    alpha = norm / (total(both[:, 256:]) * scale + RIDGE * norm)
    residual = start - alpha * (product * scale + RIDGE * start)
    parts = all_ranks(residual)
    send_features(1, parts, [residual * residual, residual * start])

    mine = lax.broadcasted_iota(jnp.int32, (1, 256), 1) // GROUP == own_slot

    def own_row(value):
        return over_rank(halves(jnp.where(mine, value, 0.0)))

    mixed_square = total(both[:, 256:])
    start, residual, product = own_row(start), own_row(residual), own_row(product)
    weights = alpha * start
    left = [blocks[8 * l + own_slot, :32] for l in range(2)]
    right = jnp.concatenate([blocks[8 * l + own_slot, 32:] for l in range(2)], axis=0)

    again = take_features(1)
    value = [to_lanes(left, right, again), products(again, again), products(again, mixed)]
    share(5, pair_2, at["c"], jnp.concatenate(value, axis=1), [other])
    norm_next, cross = take_norms(1)
    beta = norm_next / norm
    direction = residual + beta * start
    length = norm_next + 2.0 * beta * cross + beta * beta * norm
    all_of(5, pair_2.at[0]).wait_recv()
    both = pair_2[0] + pair_2[1]
    square = total(both[:, LANES:2 * LANES]) + 2.0 * beta * total(both[:, 2 * LANES:]) + beta * beta * mixed_square
    alpha = norm_next / (square * scale + RIDGE * length)
    image = (over_rank(both[:, :LANES]) + beta * product) * scale + RIDGE * direction
    out_ref[0:1] = weights + alpha * direction
    out_ref[1:2] = residual - alpha * image

    all_of(0, first.at[pl.ds(0, 15)]).wait_send()
    all_of(1, blocks.at[pl.ds(0, 6)]).wait_send()
    all_of(13, blocks.at[pl.ds(0, 6)]).wait_send()
    for d in (1, 2, 3):
        all_of(9 + d, blocks.at[0]).wait_send()
    all_of(2, second.at[pl.ds(0, 7)]).wait_send()
    for i, pair in enumerate((pair_0, pair_1, pair_2)):
        all_of(3 + i, pair.at[0]).wait_send()
    for i in range(2):
        all_of(6 + i, sums.at[i, pl.ds(0, 7)]).wait_send()
        all_of(8 + i, norms.at[i, pl.ds(0, 7)]).wait_send()


def per_device(left_factors, right_factors, left_proj, right_proj, val_ids):
    _, rows, rank, width = left_factors.shape
    left_proj = jnp.swapaxes(left_proj, 1, 2)
    right_proj = jnp.swapaxes(right_proj, 1, 2)
    ka, kb = left_proj.shape[1], right_proj.shape[1]
    val_count = val_ids.shape[0]
    total_features = ka * kb * lax.axis_size("feat")
    step = width // CHUNKS
    operands = (left_factors, right_factors, left_proj, right_proj, val_ids)
    out = pl.pallas_call(
        functools.partial(kernel, rows, rank, total_features, val_count),
        out_shape=jax.ShapeDtypeStruct((2, LANES), jnp.float32),
        in_specs=[pl.BlockSpec(memory_space=pltpu.HBM)] * 5,
        out_specs=pl.BlockSpec(memory_space=pltpu.VMEM),
        scratch_shapes=[
            pltpu.VMEM((CHUNKS, rows, rank, step), jnp.bfloat16),
            pltpu.VMEM((CHUNKS, rows, rank, step), jnp.bfloat16),
            pltpu.VMEM((ka, width), jnp.bfloat16),
            pltpu.VMEM((kb, width), jnp.bfloat16),
            pltpu.SMEM((val_count,), jnp.int32),
            pltpu.VMEM((16, ka + kb, LANES), jnp.bfloat16),
            pltpu.VMEM((2 * ka, 8 * LANES), jnp.bfloat16),
            pltpu.VMEM((2 * kb, 8 * LANES), jnp.bfloat16),
            pltpu.VMEM((16, 16, LANES), jnp.bfloat16),
            pltpu.VMEM((8, 32, LANES), jnp.bfloat16),
            pltpu.VMEM((2, 8, 32, LANES), jnp.bfloat16),
            pltpu.VMEM((2, 8, 1, 2 * LANES), jnp.float32),
            pltpu.VMEM((2, 1, 2 * LANES), jnp.float32),
            pltpu.VMEM((2, 1, 3 * LANES), jnp.float32),
            pltpu.VMEM((2, 1, 3 * LANES), jnp.float32),
            pltpu.SemaphoreType.DMA((CHUNKS, 4)),
            pltpu.SemaphoreType.DMA,
            pltpu.SemaphoreType.DMA((14,)),
            pltpu.SemaphoreType.DMA((14,)),
        ],
        compiler_params=pltpu.CompilerParams(
            collective_id=0, has_side_effects=True, vmem_limit_bytes=32 * 2**20
        ),
        name="reweight",
    )(*(pltpu.with_memory_space_constraint(a, pltpu.HBM) for a in operands))
    return out[0, :rows], out[1, :rows]


def solution(mesh):
    return jax.shard_map(
        per_device,
        mesh=mesh,
        in_specs=(
            P("feat", "ex", None, None),
            P("feat", "ex", None, None),
            P("feat", None, None),
            P("feat", None, None),
            P(),
        ),
        out_specs=(P("ex"), P("ex")),
        check_vma=False,
    )
```

```python
import functools
import math

import jax
import jax.numpy as jnp
from jax import lax
from jax.experimental import pallas as pl
from jax.experimental.pallas import tpu as pltpu
from jax.sharding import PartitionSpec as P

MESH = pl.DeviceIdType.MESH
NT = (((1,), (1,)), ((), ()))
NN = (((1,), (0,)), ((), ()))
SIZE = dict(z=8, y=4, xh=2, xl=2, c=2)
RIDGE = 0.5
CHUNKS = 4
LANES = 128
GROUP = 32


def coordinates():
    ex = lax.axis_index("ex")
    feat = lax.axis_index("feat")
    return dict(z=ex // 8, y=(ex // 2) % 4, xh=ex % 2, xl=feat // 2, c=feat % 2)


def device(at):
    return (at["z"] * 8 + at["y"] * 2 + at["xh"], at["xl"] * 2 + at["c"])


def moved(at, **steps):
    new = dict(at)
    for axis, step in steps.items():
        if not isinstance(step, int) or step:
            new[axis] = (at[axis] + step) % SIZE[axis]
    return new


def hops(y, xh, xl):
    x = 2 * xh + xl
    return min(y, 4 - y) + min(x, 4 - x)


def split(value):
    high = value.astype(jnp.bfloat16)
    low = (value - high.astype(jnp.float32)).astype(jnp.bfloat16)
    return jnp.concatenate([high, low], axis=0)


def pack(value):
    return jnp.concatenate([value[:16], value[16:]], axis=1)


def low_lanes(rows):
    return lax.broadcasted_iota(jnp.int32, (rows, LANES), 1) < LANES // 2


def side_by_side(first, second):
    low = low_lanes(16)
    top = jnp.where(low, first, pltpu.roll(second, LANES // 2, 1))
    bottom = jnp.where(low, pltpu.roll(first, LANES // 2, 1), second)
    return jnp.concatenate([top, bottom], axis=0)


def dot(a, b, dims):
    return lax.dot_general(a, b, dims, preferred_element_type=jnp.float32)


def to_features(left, right, row):
    sums = dot(split(left.astype(jnp.float32) * row), right, NT)
    return pack(sums[:32] + sums[32:])


def to_lanes(left, right, values, ranks=lambda term: term):
    low = low_lanes(32)
    both = jnp.concatenate([split(jnp.where(low, values, 0.0)), split(jnp.where(low, 0.0, values))], axis=0)
    mixed = dot(both, right, NN)
    total = ranks((mixed[:32] + mixed[32:64]) * left[0].astype(jnp.float32))
    total += ranks((mixed[64:96] + mixed[96:]) * left[1].astype(jnp.float32))
    return jnp.sum(total, axis=0, keepdims=True)


def over_rank(rows):
    rows = rows + pltpu.roll(rows, 2 * GROUP, 1)
    return rows + pltpu.roll(rows, GROUP, 1)


def total(row):
    return jnp.sum(row, axis=1, keepdims=True)


def products(a, b):
    return jnp.sum(a * b, axis=0, keepdims=True)


def halves(line):
    return line[:, :LANES] + line[:, LANES:]


def ranks_added(line):
    n = line.shape[1] // 4
    return (line[:, :n] + line[:, n:2 * n]) + (line[:, 2 * n:3 * n] + line[:, 3 * n:])


def kernel(
    rows, rank, total_features, val_count,
    lf_hbm, rf_hbm, lp_hbm, rp_hbm, ids_hbm, out_ref,
    lf, rf, lp, rp, ids, blocks, wide_left, wide_right, first, second, sums, norms, pair_0, pair_1, pair_2,
    load_sem, ids_sem, send_sem, recv_sem,
):
    at = coordinates()
    width = lf_hbm.shape[3]
    step = width // CHUNKS
    used = rows * rank
    plane_slot = at["y"] * 2 + at["xh"]
    near = at["z"] % 2
    own_slot = at["xh"]
    slot = at["xl"] * 8 + own_slot
    group_slot = at["y"] * 2 + near

    along_z = [moved(at, z=d) for d in (4, 3, 5, 2, 6, 1, 7)]
    plane = [(y, xh, xl) for y in range(4) for xh in range(2) for xl in range(2) if y or xh or xl]
    plane = [moved(at, y=y, xh=xh, xl=xl) for y, xh, xl in sorted(plane, key=lambda o: -hops(*o))]
    other = moved(at, c=1)
    along_x = [moved(at, xh=xh, xl=xl) for xh, xl in ((1, 0), (0, 1), (1, 1))]
    twins = [moved(at, y=y, z=1 - 2 * near) for y in (2, 1, 3, 0)]
    sharers = [twins[0], moved(at, y=2)] + twins[1:3] + [moved(at, y=1), moved(at, y=3), twins[3]]
    barrier = pltpu.get_barrier_semaphore()
    order = along_z[:1] + plane[:1] + along_z[1:3] + plane[1:5] + twins[:1]
    rest = along_z[3:] + plane[5:] + twins[1:3] + [other]

    def greet(peers):
        for peer in peers:
            pl.semaphore_signal(barrier, inc=1, device_id=device(peer), device_id_type=MESH)

    greet(order)

    load_ids = pltpu.make_async_copy(ids_hbm, ids, ids_sem)
    load_ids.start()
    loads = []
    for i in range(CHUNKS):
        part = pl.ds(i * step, step)
        group = [
            pltpu.make_async_copy(lp_hbm.at[0, :, part], lp.at[:, part], load_sem.at[i, 0]),
            pltpu.make_async_copy(lf_hbm.at[0, :, :, part], lf.at[i], load_sem.at[i, 1]),
            pltpu.make_async_copy(rp_hbm.at[0, :, part], rp.at[:, part], load_sem.at[i, 2]),
            pltpu.make_async_copy(rf_hbm.at[0, :, :, part], rf.at[i], load_sem.at[i, 3]),
        ]
        for copy in group:
            copy.start()
        loads.append(group)
    greet(rest)

    lane = lax.broadcasted_iota(jnp.int32, (8, LANES), 1) % GROUP
    own_id = jnp.where(lane < rows, (at["z"] * 8 + plane_slot) * rows + lane, -1)
    load_ids.wait()

    def count(i, counts):
        for j in range(8):
            counts = counts + jnp.where(own_id == ids[i * 8 + j], 1.0, 0.0)
        return counts

    counts = lax.fori_loop(0, val_count // 8, count, jnp.zeros((8, LANES), jnp.float32))[:1]

    left_part = jnp.zeros((32, used), jnp.float32)
    right_part = jnp.zeros((64, used), jnp.float32)
    for i in range(CHUNKS):
        for copy in loads[i]:
            copy.wait()
        part = slice(i * step, (i + 1) * step)
        left_part += dot(lp[:, part], lf[i].reshape(used, step), NT)
        right_part += dot(rp[:, part], rf[i].reshape(used, step), NT)
    own = jnp.concatenate([left_part, right_part], axis=0).astype(jnp.bfloat16)
    source = lax.broadcasted_iota(jnp.int32, (used, LANES), 0)
    goal = lax.broadcasted_iota(jnp.int32, (used, LANES), 1)
    place = jnp.where((source // rank == goal % GROUP) & (source % rank == goal // GROUP), 1.0, 0.0)
    own = dot(own, place.astype(jnp.bfloat16), NN).astype(jnp.bfloat16)
    blocks[slot] = own

    def send(stage, source, goal, peers):
        for peer in peers:
            pltpu.make_async_remote_copy(
                src_ref=source, dst_ref=goal, send_sem=send_sem.at[stage], recv_sem=recv_sem.at[stage],
                device_id=device(peer), device_id_type=MESH,
            ).start()

    def all_of(stage, view):
        return pltpu.make_async_remote_copy(
            src_ref=view, dst_ref=view, send_sem=send_sem.at[stage], recv_sem=recv_sem.at[stage],
            device_id=device(other), device_id_type=MESH,
        )

    def share(stage, buffer, index, value, peers):
        buffer[index] = value
        send(stage, buffer.at[index], buffer.at[index], peers)

    target = to_features(own[:32], own[32:], counts)
    pl.semaphore_wait(barrier, len(order) + len(rest))
    place_of = {1: 1, 3: 2, 2: 3}
    index = at["xl"] * 8 + plane_slot
    first[index] = target.astype(first.dtype)
    send(0, first.at[index], first.at[index], plane[:5])
    for d in (2, 1, 3):
        send(9 + d, blocks.at[slot], blocks.at[slot + 2 * place_of[d]], [moved(at, z=2 * d)])
    send(0, first.at[index], first.at[index], plane[5:])
    send(1, blocks.at[slot], blocks.at[slot], along_x)

    def forward(d):
        come = slot + 2 * place_of[d]
        all_of(9 + d, blocks.at[come]).wait_recv()
        send(1 if d == 1 else 13, blocks.at[come], blocks.at[come], along_x)

    def lay_out(h):
        for l in range(2):
            four = [blocks[8 * l + 4 * h + j].astype(jnp.float32) for j in range(4)]
            for r in range(4):
                moves = [pltpu.roll(four[j], GROUP * ((j - r) % 4), 1) if j != r else four[j] for j in range(4)]
                value = jnp.where(
                    segment < 2, jnp.where(segment == 0, moves[0], moves[1]),
                    jnp.where(segment == 2, moves[2], moves[3]),
                )
                lanes = slice(256 * r + LANES * h, 256 * r + LANES * h + LANES)
                wide_left[pl.ds(32 * l, 32), lanes] = value[:32].astype(jnp.bfloat16)
                wide_right[pl.ds(64 * l, 64), lanes] = value[32:].astype(jnp.bfloat16)

    segment = lax.broadcasted_iota(jnp.int32, (96, LANES), 1) // GROUP
    forward(1)
    forward(3)
    all_of(0, first.at[pl.ds(0, 15)]).wait_recv()
    target = [jnp.sum(first[pl.ds(8 * l, 8)].astype(jnp.float32), axis=0) for l in range(2)]
    share(2, second, at["z"], side_by_side(*target).astype(second.dtype), along_z)
    forward(2)
    all_of(1, blocks.at[pl.ds(0, 6)]).wait_recv()
    lay_out(0)
    all_of(13, blocks.at[pl.ds(0, 6)]).wait_recv()
    lay_out(1)
    left = [wide_left[:32], wide_left[32:]]
    right = wide_right[...]
    all_of(2, second.at[pl.ds(0, 7)]).wait_recv()
    target = jnp.sum(second[...].astype(jnp.float32), axis=0)

    def all_ranks(line):
        line = jnp.concatenate([line] * 4, axis=1)
        both = jnp.concatenate([split(left[l].astype(jnp.float32) * line) for l in range(2)], axis=0)
        parts = dot(both, right, NT)
        return jnp.where(low_lanes(32), parts[:32] + parts[32:64], parts[64:96] + parts[96:])

    def send_features(index, values, scalars):
        share(6 + index, sums.at[index], group_slot, values.astype(jnp.bfloat16), sharers)
        share(8 + index, norms.at[index], group_slot, jnp.concatenate([halves(s) for s in scalars], axis=1), sharers)

    def take_features(index):
        all_of(6 + index, sums.at[index, pl.ds(0, 7)]).wait_recv()
        return jnp.sum(sums[index].astype(jnp.float32), axis=0)

    def take_norms(index):
        all_of(8 + index, norms.at[index, pl.ds(0, 7)]).wait_recv()
        whole = jnp.sum(norms[index], axis=0)
        return total(whole[:, :LANES]), total(whole[:, LANES:])

    scale = 1.0 / (rank * total_features)
    align_scale = math.sqrt(val_count / total_features) / (val_count * rank)

    share(3, pair_0, at["c"], to_lanes(left, right, target, ranks_added), [other])
    all_of(3, pair_0.at[0]).wait_recv()
    start = (pair_0[0] + pair_0[1]) * align_scale
    start_parts = all_ranks(start)
    send_features(0, start_parts, [start * start, start])
    mixed = take_features(0)

    value = [to_lanes(left, right, mixed, ranks_added), products(mixed, mixed)]
    share(4, pair_1, at["c"], jnp.concatenate(value, axis=1), [other])
    norm, _ = take_norms(0)
    all_of(4, pair_1.at[0]).wait_recv()
    both = pair_1[0] + pair_1[1]
    product = both[:, :256]
    alpha = norm / (total(both[:, 256:]) * scale + RIDGE * norm)
    residual = start - alpha * (product * scale + RIDGE * start)
    parts = all_ranks(residual)
    send_features(1, parts, [residual * residual, residual * start])

    mine = lax.broadcasted_iota(jnp.int32, (1, 256), 1) // GROUP == own_slot

    def own_row(value):
        return over_rank(halves(jnp.where(mine, value, 0.0)))

    mixed_square = total(both[:, 256:])
    start, residual, product = own_row(start), own_row(residual), own_row(product)
    weights = alpha * start
    left = [blocks[8 * l + own_slot, :32] for l in range(2)]
    right = jnp.concatenate([blocks[8 * l + own_slot, 32:] for l in range(2)], axis=0)

    all_of(0, first.at[pl.ds(0, 15)]).wait_send()
    all_of(1, blocks.at[pl.ds(0, 6)]).wait_send()
    all_of(13, blocks.at[pl.ds(0, 6)]).wait_send()
    for d in (1, 2, 3):
        all_of(9 + d, blocks.at[0]).wait_send()
    all_of(2, second.at[pl.ds(0, 7)]).wait_send()
    all_of(3, pair_0.at[0]).wait_send()
    all_of(4, pair_1.at[0]).wait_send()
    all_of(6, sums.at[0, pl.ds(0, 7)]).wait_send()
    all_of(8, norms.at[0, pl.ds(0, 7)]).wait_send()

    again = take_features(1)
    value = [to_lanes(left, right, again), products(again, again), products(again, mixed)]
    share(5, pair_2, at["c"], jnp.concatenate(value, axis=1), [other])
    norm_next, cross = take_norms(1)
    beta = norm_next / norm
    direction = residual + beta * start
    length = norm_next + 2.0 * beta * cross + beta * beta * norm
    all_of(7, sums.at[1, pl.ds(0, 7)]).wait_send()
    all_of(9, norms.at[1, pl.ds(0, 7)]).wait_send()
    all_of(5, pair_2.at[0]).wait_recv()
    both = pair_2[0] + pair_2[1]
    square = total(both[:, LANES:2 * LANES]) + 2.0 * beta * total(both[:, 2 * LANES:]) + beta * beta * mixed_square
    alpha = norm_next / (square * scale + RIDGE * length)
    image = (over_rank(both[:, :LANES]) + beta * product) * scale + RIDGE * direction
    out_ref[0:1] = weights + alpha * direction
    out_ref[1:2] = residual - alpha * image
    all_of(5, pair_2.at[0]).wait_send()


def per_device(left_factors, right_factors, left_proj, right_proj, val_ids):
    _, rows, rank, width = left_factors.shape
    left_proj = jnp.swapaxes(left_proj, 1, 2)
    right_proj = jnp.swapaxes(right_proj, 1, 2)
    ka, kb = left_proj.shape[1], right_proj.shape[1]
    val_count = val_ids.shape[0]
    total_features = ka * kb * lax.axis_size("feat")
    step = width // CHUNKS
    operands = (left_factors, right_factors, left_proj, right_proj, val_ids)
    out = pl.pallas_call(
        functools.partial(kernel, rows, rank, total_features, val_count),
        out_shape=jax.ShapeDtypeStruct((2, LANES), jnp.float32),
        in_specs=[pl.BlockSpec(memory_space=pltpu.HBM)] * 5,
        out_specs=pl.BlockSpec(memory_space=pltpu.VMEM),
        scratch_shapes=[
            pltpu.VMEM((CHUNKS, rows, rank, step), jnp.bfloat16),
            pltpu.VMEM((CHUNKS, rows, rank, step), jnp.bfloat16),
            pltpu.VMEM((ka, width), jnp.bfloat16),
            pltpu.VMEM((kb, width), jnp.bfloat16),
            pltpu.SMEM((val_count,), jnp.int32),
            pltpu.VMEM((16, ka + kb, LANES), jnp.bfloat16),
            pltpu.VMEM((2 * ka, 8 * LANES), jnp.bfloat16),
            pltpu.VMEM((2 * kb, 8 * LANES), jnp.bfloat16),
            pltpu.VMEM((16, 16, LANES), jnp.bfloat16),
            pltpu.VMEM((8, 32, LANES), jnp.bfloat16),
            pltpu.VMEM((2, 8, 32, LANES), jnp.bfloat16),
            pltpu.VMEM((2, 8, 1, 2 * LANES), jnp.float32),
            pltpu.VMEM((2, 1, 2 * LANES), jnp.float32),
            pltpu.VMEM((2, 1, 3 * LANES), jnp.float32),
            pltpu.VMEM((2, 1, 3 * LANES), jnp.float32),
            pltpu.SemaphoreType.DMA((CHUNKS, 4)),
            pltpu.SemaphoreType.DMA,
            pltpu.SemaphoreType.DMA((14,)),
            pltpu.SemaphoreType.DMA((14,)),
        ],
        compiler_params=pltpu.CompilerParams(
            collective_id=0, has_side_effects=True, vmem_limit_bytes=32 * 2**20
        ),
        name="reweight",
    )(*(pltpu.with_memory_space_constraint(a, pltpu.HBM) for a in operands))
    return out[0, :rows], out[1, :rows]


def solution(mesh):
    return jax.shard_map(
        per_device,
        mesh=mesh,
        in_specs=(
            P("feat", "ex", None, None),
            P("feat", "ex", None, None),
            P("feat", None, None),
            P("feat", None, None),
            P(),
        ),
        out_specs=(P("ex"), P("ex")),
        check_vma=False,
    )
```
